512 devices in a mesh: grp: 16 (over x, y), trn: 32 (over z, core).
Axes of the slice: x: 4, y: 4, z: 16, core: 2. Of those that a mesh axis runs over, the one named last changes fastest.
Arguments:
- features: bfloat16 [131072, 1024], P(('grp', 'trn')), may hold values from -24 to 24
- query_rows: bfloat16 [131072, 512], P(('grp', 'trn')), may hold values from -6 to 6
- key_rows: bfloat16 [131072, 512], P(('grp', 'trn')), may hold values from -6 to 6
- w_value: bfloat16 [1024, 512], P(('grp', 'trn')), may hold values from -0.1875 to 0.1875
- cotangent: bfloat16 [131072, 512], P(('grp', 'trn')), may hold values from -6 to 6
- station: int32 [131072], P(('grp', 'trn')), may hold values from 47 to 8191, as said below
- bucket: int32 [131072], P(('grp', 'trn')), may hold values from 0 to 15
- slot_index: int32 [131072], P(('grp', 'trn')), may hold values from 0 to 8191, as said below
Outputs:
- mixed_out: bfloat16 [131072, 512], P(('grp', 'trn'))
- grad_features: bfloat16 [131072, 1024], P(('grp', 'trn'))
- grad_query: bfloat16 [131072, 512], P(('grp', 'trn'))
- grad_key: bfloat16 [131072, 512], P(('grp', 'trn'))
- grad_weight: float32 [1024, 512], P(('grp', 'trn'))
The draws below stay inside these ranges and needn't reach their ends.
Inputs may be any that keep to these rules, and one draw needn't show every extreme that they name: Within each group of 8192 consecutive rows, slot_index is a permutation of the group's positions; of the rows of one device exactly 8 fall in each block of 256 consecutive positions. Along each group's station-major order, the rows of one station are consecutive, 1 to 48 of them, one station exactly 48; a station's id is the station-major position of its last row.
All inputs are finite; a program needn't handle non-finite values.
Results may differ from the reference program's by a relative error of at most 0.018.
Values may be sent and summed in bfloat16 or wider, within the bound.
A program may use at most 64 MiB of HBM per device.

```python
import jax
import jax.numpy as jnp
from jax import lax

D = 1024
HEADS = 8
HDIM = 64
HD = 512
S = 256
WIN = 128
RUN = 48
BUCKETS = 16
R_DEV = 256
ROWS_GRP = 8192
ROWS = 131072


def pair_rows(key):
    first = jnp.clip(jax.random.normal(jax.random.fold_in(key, 1), (ROWS, HD), jnp.float32), -6.0, 6.0)
    second = jnp.clip(jax.random.normal(jax.random.fold_in(key, 2), (ROWS, HD), jnp.float32), -6.0, 6.0)
    return (first, second)


def draw_query_rows(key, part):
    return pair_rows(key)[0].astype(jnp.bfloat16)


def draw_key_rows(key, part):
    return pair_rows(key)[1].astype(jnp.bfloat16)


def slot_table(key):
    groups = ROWS // ROWS_GRP
    members = ROWS_GRP // R_DEV
    per_peer = R_DEV // members

    def ranking(subkey):
        scores = jax.random.randint(subkey, (groups, members, R_DEV), 0, 1 << 20) * R_DEV + jnp.arange(R_DEV)
        return jnp.argsort(scores, axis=-1)
    source_order = ranking(jax.random.fold_in(key, 101))
    source_rank = jnp.argsort(source_order, axis=-1)
    target_order = ranking(jax.random.fold_in(key, 102))
    target_dev = source_rank // per_peer
    within = source_rank % per_peer
    group_ids = jnp.arange(groups)[:, None, None]
    sender = jnp.arange(members)[None, :, None]
    position = target_order[group_ids, target_dev, sender * per_peer + within]
    return (target_dev * R_DEV + position).reshape(ROWS).astype(jnp.int32)


def draw_slot_index(key, part):
    return slot_table(key)


def draw_station(key, part):
    slots = slot_table(key)
    groups = ROWS // ROWS_GRP
    lengths = jax.random.randint(jax.random.fold_in(key, 103), (groups, ROWS_GRP), 1, RUN + 1)
    lengths = lengths.at[:, 0].set(RUN)
    ends = jnp.cumsum(lengths, axis=-1)
    positions = jnp.arange(ROWS_GRP)
    segment = jax.vmap(lambda edges: jnp.searchsorted(edges, positions, side='right'))(ends)
    last_row = jnp.minimum(jnp.take_along_axis(ends, segment, axis=-1) - 1, ROWS_GRP - 1)
    group_of_row = jnp.arange(ROWS) // ROWS_GRP
    return last_row[group_of_row, slots].astype(jnp.int32)


def place_ends(values, key, low, high):
    longest = values.shape.index(max(values.shape))
    spots = []
    for shift in (0, 1):
        where = [jax.random.randint(jax.random.fold_in(key, axis), (), 0, length) for axis, length in enumerate(values.shape)]
        where[longest] = (where[longest] + shift) % values.shape[longest]
        spots.append(tuple(where))
    return values.at[spots[0]].set(low).at[spots[1]].set(high)


def spiked(values, own_key, source, target, shards_of, factor):
    owner, partner = [(jnp.arange(values.shape[dim]) // (values.shape[dim] // shards_of)).reshape([-1 if axis == dim else 1 for axis in range(values.ndim)]) for dim in (source, target)]
    chosen = jax.random.permutation(own_key, shards_of)[partner]
    strong = (owner == chosen) | (owner == (partner + shards_of // 2) % shards_of)
    return jnp.where(strong, factor * values, values)


def levels(own_key, extent, shards, smallest, top_value):
    level, own = 1.0, jax.random.fold_in(own_key, 6)
    for dim, blocks in shards:
        steps = jnp.exp(jax.random.uniform(jax.random.fold_in(own, dim), (blocks,), jnp.float32, smallest / len(shards), top_value / len(shards)))
        level = level * jnp.repeat(steps, extent[dim] // blocks).reshape([-1 if axis == dim else 1 for axis in range(len(extent))])
    return level


def noise(key, extent, width, bound, shards=(), held_as=jnp.bfloat16):
    gain = levels(key, extent, shards, -0.22, 0.18) if shards else 1.0
    values = jax.random.normal(key, extent, jnp.float32) * width * gain
    return jnp.minimum(jnp.maximum(values, -bound), bound).astype(held_as)


def bell_draw_with(own_key, shape, width, bound, pieces, heavy, kind=jnp.bfloat16):
    drawn = width * jax.random.normal(own_key, shape, jnp.float32)
    if pieces:
        drawn = drawn * levels(own_key, shape, pieces, -0.22, 0.18)
    return jnp.clip(spiked(drawn, jax.random.fold_in(own_key, 3), *heavy), -bound, bound).astype(kind)


def setup_inputs(seed: int = 0) -> dict:
    seeds = jax.random.split(jax.random.key(seed), 9)
    features = bell_draw_with(seeds[0], (ROWS, D), 1.0, 24.0, ((0, 512),), (0, 1, 512, 6.0))
    query_rows = draw_query_rows(jax.random.fold_in(seeds[8], 71), 0)
    key_rows = draw_key_rows(jax.random.fold_in(seeds[8], 71), 0)
    w_value = noise(seeds[3], (D, HD), D ** -0.5, 0.1875, ((0, 512),))
    cotangent = noise(seeds[4], (ROWS, HD), 1.0, 6.0, ((0, 512),))
    station = draw_station(jax.random.fold_in(seeds[8], 71), 0)
    bucket = place_ends(jax.random.randint(seeds[6], (ROWS,), 0, BUCKETS), jax.random.fold_in(seeds[6], 1), 0, BUCKETS - 1).astype(jnp.int32)
    slot_index = draw_slot_index(jax.random.fold_in(seeds[8], 71), 0)
    return dict(features=features, query_rows=query_rows, key_rows=key_rows, w_value=w_value, cotangent=cotangent, station=station, bucket=bucket, slot_index=slot_index)


def attend(query_part, key_part, value_part, allowed, factor):
    scores = jnp.einsum("blhd,bmhd->bhlm", query_part.astype(jnp.float32), key_part.astype(jnp.float32)) * factor
    scores = jnp.where(allowed[:, None], scores, -1e30)
    top_score = jnp.max(scores, -1, keepdims=True)
    raised = jnp.exp(scores - top_score)
    weights = raised / jnp.sum(raised, -1, keepdims=True)
    weights_half = weights.astype(jnp.bfloat16)
    output = jnp.einsum("bhlm,bmhd->blhd", weights_half.astype(jnp.float32), value_part.astype(jnp.float32))
    return output.astype(jnp.bfloat16), weights, weights_half


def attend_back(query_part, key_part, value_part, allowed, grad_out, factor):
    unused, weights, weights_half = attend(query_part, key_part, value_part, allowed, factor)
    grad_weights = jnp.einsum("blhd,bmhd->bhlm", grad_out.astype(jnp.float32), value_part.astype(jnp.float32))
    row_dot = jnp.sum(weights * grad_weights, -1, keepdims=True)
    grad_scores = (weights * (grad_weights - row_dot) * factor).astype(jnp.bfloat16).astype(jnp.float32)
    grad_query = jnp.einsum("bhlm,bmhd->blhd", grad_scores, key_part.astype(jnp.float32))
    grad_key = jnp.einsum("bhlm,blhd->bmhd", grad_scores, query_part.astype(jnp.float32))
    grad_value = jnp.einsum("bhlm,blhd->bmhd", weights_half.astype(jnp.float32), grad_out.astype(jnp.float32))
    return grad_query, grad_key, grad_value


def reference(features, query_rows, key_rows, w_value, cotangent, station, bucket, slot_index):
    factor = HDIM ** -0.5
    values = jnp.dot(features, w_value, preferred_element_type=jnp.float32).astype(jnp.bfloat16)

    def by_train(array):
        return array.reshape(ROWS // (8 * S), 8, S, HEADS, HDIM)

    causal = jnp.broadcast_to(jnp.tril(jnp.ones((S, S), dtype=jnp.bool_)), (8, S, S))

    def stop_forward(parts):
        return attend(parts[0], parts[1], parts[2], causal, factor)[0]

    context = lax.map(stop_forward, (by_train(query_rows), by_train(key_rows), by_train(values))).reshape(ROWS, HD)
    row_ids = jnp.arange(ROWS, dtype=jnp.int32)
    target = (row_ids // ROWS_GRP) * ROWS_GRP + slot_index.astype(jnp.int32)
    source = jnp.zeros((ROWS,), jnp.int32).at[target].set(row_ids)

    def by_window(array):
        return array[source].reshape(ROWS // (8 * WIN), 8, WIN, HEADS, HDIM)

    station_major = station[source].reshape(ROWS // (8 * WIN), 8, WIN)
    bucket_major = bucket[source].reshape(ROWS // (8 * WIN), 8, WIN)

    def window_mask(stations, buckets):
        return (stations[:, :, None] == stations[:, None, :]) & (buckets[:, None, :] <= buckets[:, :, None])

    def window_forward(parts):
        allowed = window_mask(parts[3], parts[4])
        return attend(parts[0], parts[1], parts[2], allowed, factor)[0]

    window_parts = (by_window(query_rows), by_window(key_rows), by_window(context), station_major, bucket_major)
    mixed = lax.map(window_forward, window_parts).reshape(ROWS, HD)
    mixed_out = mixed[target]

    def window_backward(parts):
        allowed = window_mask(parts[3], parts[4])
        grads = attend_back(parts[0], parts[1], parts[2], allowed, parts[5], factor)
        return tuple(item.astype(jnp.bfloat16) for item in grads)

    win_query, win_key, win_context = lax.map(window_backward, window_parts + (by_window(cotangent),))
    win_query = win_query.reshape(ROWS, HD)[target]
    win_key = win_key.reshape(ROWS, HD)[target]
    grad_context = win_context.reshape(ROWS, HD)[target]

    def stop_backward(parts):
        return attend_back(parts[0], parts[1], parts[2], causal, parts[3], factor)

    stop_query, stop_key, stop_value = lax.map(stop_backward, (by_train(query_rows), by_train(key_rows), by_train(values), by_train(grad_context)))
    grad_value = stop_value.reshape(ROWS, HD).astype(jnp.bfloat16)
    grad_query = (stop_query.reshape(ROWS, HD) + win_query.astype(jnp.float32)).astype(jnp.bfloat16)
    grad_key = (stop_key.reshape(ROWS, HD) + win_key.astype(jnp.float32)).astype(jnp.bfloat16)
    grad_features = jnp.dot(grad_value, w_value.T, preferred_element_type=jnp.float32).astype(jnp.bfloat16)
    grad_weight = jnp.dot(features.T, grad_value, preferred_element_type=jnp.float32) * (ROWS ** -0.5)
    return (mixed_out, grad_features, grad_query, grad_key, grad_weight)
```

```python
import functools

import jax
import jax.numpy as jnp
from jax import lax
from jax.experimental import pallas as pl
from jax.experimental.pallas import tpu as pltpu
from jax.sharding import PartitionSpec as P

MESH = pl.DeviceIdType.MESH
BF16 = jnp.bfloat16
F32 = jnp.float32
I32 = jnp.int32
HEADS = 8
HDIM = 64
HD = 512
D = 1024
R = 256
WIN = 128
MEMBERS = 32
GROUPS = 16
CHIPS = 16
NEG = -1e30


def dot(a, b):
    return lax.dot_general(a, b, (((1,), (0,)), ((), ())), preferred_element_type=F32)


def dot_nt(a, b):
    return lax.dot_general(a, b, (((1,), (1,)), ((), ())), preferred_element_type=F32)


def dot_tn(a, b):
    return lax.dot_general(a, b, (((0,), (0,)), ((), ())), preferred_element_type=F32)


def iota(shape, dim):
    return lax.broadcasted_iota(I32, shape, dim)


def to_col(row):
    eye = iota((R, R), 0) == iota((R, R), 1)
    return jnp.sum(jnp.where(eye, jnp.broadcast_to(row, (R, R)), 0), axis=1, keepdims=True)


def to_row(col):
    eye = iota((R, R), 0) == iota((R, R), 1)
    return jnp.sum(jnp.where(eye, jnp.broadcast_to(col, (R, R)), 0), axis=0, keepdims=True)


def pack(rows):
    cut = rows.reshape(MEMBERS, 8, HD)
    return jnp.concatenate([cut[:, :, : HD // 2], cut[:, :, HD // 2 :]], axis=1).reshape(2 * R, HD // 2).astype(BF16)


def unpack(block):
    cut = block.astype(F32).reshape(MEMBERS, 16, HD // 2)
    low = cut[:, :8].reshape(R, HD // 2)
    high = cut[:, 8:].reshape(R, HD // 2)
    return jnp.concatenate([low, high], axis=1).astype(BF16)


def softmax(scores):
    top = jnp.max(scores, axis=1, keepdims=True)
    raised = jnp.exp(scores - top)
    return raised * (1.0 / jnp.sum(raised, axis=1, keepdims=True))


def kernel(
    feat, query, key, w_part, cot, station, bucket, slot,
    mixed_o, gfeat_o, gq_o, gk_o, gw_o,
    order, restore, bias, stop_p, win_p,
    send_a, recv_a, send_m, recv_m, send_c, recv_c, send_d, recv_d, send_r, recv_r,
    w_send, w_recv, w_rows, w_full,
    vals, ctx, grad_c, grad_v, stop_q, stop_k,
    qw, kw, vw, dw, out_m, out_q, out_k,
    gw_own, rs0_send, rs0_recv, rs1_send, rs1_recv, rs2_send, rs2_recv, rs3_send, rs3_recv,
    sems,
):
    grp = lax.axis_index("grp")
    trn = lax.axis_index("trn")
    chip = trn // 2
    core = trn % 2
    sibling = chip * 2 + (1 - core)

    def member(step):
        return lax.rem(trn + step, MEMBERS)

    def group(step):
        return lax.rem(grp + step, GROUPS)

    barrier = pltpu.get_barrier_semaphore()

    @pl.loop(1, MEMBERS)
    def _(step):
        pl.semaphore_signal(barrier, inc=1, device_id=(grp, member(step)), device_id_type=MESH)

    @pl.loop(1, GROUPS)
    def _(step):
        pl.semaphore_signal(barrier, inc=1, device_id=(group(step), trn), device_id_type=MESH)

    def blocks(ref, who, rows):
        return ref.at[pl.ds(pl.multiple_of(who * rows, rows), rows)]

    def exchange(send, recv, rows, ssem, rsem):
        pltpu.make_async_copy(blocks(send, trn, rows), blocks(recv, trn, rows), sems.at[rsem]).start()

        @pl.loop(1, MEMBERS)
        def _(step):
            peer = member(step)
            pltpu.make_async_remote_copy(
                src_ref=blocks(send, peer, rows), dst_ref=blocks(recv, trn, rows),
                send_sem=sems.at[ssem], recv_sem=sems.at[rsem],
                device_id=(grp, peer), device_id_type=MESH,
            ).start()

    def wait_for(ref, sem):
        pltpu.make_async_copy(ref, ref, sems.at[sem]).wait()

    def arrived(recv, rsem):
        wait_for(recv, rsem)

    def sent(send, rows, ssem):
        wait_for(send.at[pl.ds(0, (MEMBERS - 1) * rows)], ssem)

    slot_row = slot[...]
    goal_row = slot_row // R
    goal_col = to_col(goal_row)
    same = (goal_col == goal_row) & (iota((R, R), 0) < iota((R, R), 1))
    rank_row = jnp.sum(jnp.where(same, 1, 0), axis=0, keepdims=True)
    pos_row = goal_row * 8 + rank_row
    pos_col = to_col(pos_row)
    picks = iota((R, R), 0) == pos_row
    order[...] = jnp.where(picks, 1.0, 0.0).astype(BF16)
    restore[...] = jnp.where(pos_col == iota((R, R), 1), 1.0, 0.0).astype(BF16)

    half = HD // 2
    send_a[:, 0:half] = pack(dot(order[...], query[...]))
    send_a[:, half : 2 * half] = pack(dot(order[...], key[...]))
    send_a[:, 2 * half :] = pack(dot(order[...], cot[...]))

    lane = iota((R, 128), 1)
    within = iota((R, 128), 0) % 8

    def sorted_col(row):
        return jnp.sum(jnp.where(picks, jnp.broadcast_to(row, (R, R)), 0), axis=1, keepdims=True)

    place_col = sorted_col(slot_row % R)
    station_col = sorted_col(station[...])
    bucket_col = sorted_col(bucket[...])
    meta = (
        jnp.where(lane == within, place_col, 0)
        + jnp.where(lane == within + 8, station_col, 0)
        + jnp.where(lane == within + 16, bucket_col, 0)
    )
    send_m[...] = jnp.sum(meta.reshape(MEMBERS, 8, 128), axis=1, keepdims=True)
    w_send[...] = w_part[...].astype(F32)

    pl.semaphore_wait(barrier, MEMBERS - 1 + GROUPS - 1)

    near = trn // 16
    index = lax.rem(trn, 16)
    own_near = core == near

    @pl.when(own_near)
    def _():
        pltpu.make_async_copy(w_send, w_recv.at[index], sems.at[1]).start()

    @pl.when(jnp.logical_not(own_near))
    def _():
        pltpu.make_async_remote_copy(
            src_ref=w_send, dst_ref=w_recv.at[index], send_sem=sems.at[0], recv_sem=sems.at[1],
            device_id=(grp, chip * 2 + near), device_id_type=MESH,
        ).start()

    @pl.loop(1, CHIPS)
    def _(step):
        pltpu.make_async_remote_copy(
            src_ref=w_send, dst_ref=w_recv.at[index], send_sem=sems.at[0], recv_sem=sems.at[1],
            device_id=(grp, lax.rem(chip + step, CHIPS) * 2 + near), device_id_type=MESH,
        ).start()

    def all_blocks_m(step):
        peer = member(step)
        pltpu.make_async_remote_copy(
            src_ref=send_m.at[peer], dst_ref=recv_m.at[trn], send_sem=sems.at[4], recv_sem=sems.at[5],
            device_id=(grp, peer), device_id_type=MESH,
        ).start()

    pltpu.make_async_copy(send_m.at[trn], recv_m.at[trn], sems.at[5]).start()
    pl.loop(1, MEMBERS)(all_blocks_m)
    exchange(send_a, recv_a, 16, 2, 3)

    arrived(w_recv, 1)
    for step in range(CHIPS):
        w_rows[2 * step : 2 * step + 2, :] = w_recv[step]
    w_full[grp, core] = w_rows[...].astype(BF16)

    @pl.loop(1, GROUPS)
    def _(step):
        pltpu.make_async_remote_copy(
            src_ref=w_full.at[grp, core], dst_ref=w_full.at[grp, core], send_sem=sems.at[6], recv_sem=sems.at[7],
            device_id=(group(step), trn), device_id_type=MESH,
        ).start()

    low_lane = iota((R, 128), 1) < HDIM

    def heads_of(ref, pair):
        part = ref[:, pl.ds(pl.multiple_of(pair * 128, 128), 128)]
        zero = jnp.zeros_like(part)
        return part, jnp.where(low_lane, part, zero), jnp.where(low_lane, zero, part)

    def cols(pair):
        return (slice(None), pl.ds(pl.multiple_of(pair * 128, 128), 128))

    def weights_into(target, q_ref, k_ref):
        @pl.loop(0, HEADS // 2)
        def _(pair):
            k_pair = k_ref[cols(pair)]
            _, *q_heads = heads_of(q_ref, pair)
            for head in range(2):
                scores = dot_nt(q_heads[head], k_pair) * (HDIM ** -0.5) + bias[...]
                target[2 * pair + head] = softmax(scores).astype(BF16)

    bias[...] = jnp.where(iota((R, R), 1) <= iota((R, R), 0), 0.0, NEG)
    weights_into(stop_p, query, key)

    wait_for(w_full.at[pl.ds(0, GROUPS - 1), core], 7)
    wait_for(w_full.at[pl.ds(0, GROUPS - 1), core], 6)
    swap_w = pltpu.make_async_remote_copy(
        src_ref=w_full.at[:, core], dst_ref=w_full.at[:, core], send_sem=sems.at[8], recv_sem=sems.at[9],
        device_id=(grp, sibling), device_id_type=MESH,
    )
    swap_w.start()
    swap_w.wait()

    weight = w_full[...].reshape(D, HD)
    vals[...] = dot(feat[...], weight).astype(BF16)

    def attend(p_ref, v_ref, out_ref):
        @pl.loop(0, HEADS // 2)
        def _(pair):
            v_pair = v_ref[cols(pair)]
            first = dot(p_ref[2 * pair], v_pair)
            second = dot(p_ref[2 * pair + 1], v_pair)
            out_ref[cols(pair)] = jnp.where(low_lane, first, second).astype(out_ref.dtype)

    def attend_value_back(p_ref, d_ref, out_ref):
        @pl.loop(0, HEADS // 2)
        def _(pair):
            d_pair = d_ref[cols(pair)]
            first = dot_tn(p_ref[2 * pair], d_pair)
            second = dot_tn(p_ref[2 * pair + 1], d_pair)
            out_ref[cols(pair)] = jnp.where(low_lane, first, second).astype(out_ref.dtype)

    def attend_back(p_ref, q_ref, k_ref, v_ref, d_ref, dq_ref, dk_ref):
        @pl.loop(0, HEADS // 2)
        def _(pair):
            q_pair, k_pair, v_pair = q_ref[cols(pair)], k_ref[cols(pair)], v_ref[cols(pair)]
            _, *d_heads = heads_of(d_ref, pair)
            dq, dk = [], []
            for head in range(2):
                weights = p_ref[2 * pair + head].astype(F32)
                grad = dot_nt(d_heads[head], v_pair)
                row_dot = jnp.sum(weights * grad, axis=1, keepdims=True)
                grad = (weights * (grad - row_dot)).astype(BF16)
                dq.append(dot(grad, k_pair))
                dk.append(dot_tn(grad, q_pair))
            factor = HDIM ** -0.5
            dq_ref[cols(pair)] = (jnp.where(low_lane, dq[0], dq[1]) * factor).astype(dq_ref.dtype)
            dk_ref[cols(pair)] = (jnp.where(low_lane, dk[0], dk[1]) * factor).astype(dk_ref.dtype)

    attend(stop_p, vals, ctx)
    send_c[...] = pack(dot(order[...], ctx[...]))
    exchange(send_c, recv_c, 16, 10, 11)

    arrived(recv_m, 5)
    got = jnp.broadcast_to(recv_m[...], (MEMBERS, 8, 128)).reshape(R, 128)

    def field(number):
        return jnp.sum(jnp.where(lane == within + 8 * number, got, 0), axis=1, keepdims=True)

    piece = field(1) * 2 + field(0) // WIN
    buckets = field(2)
    allowed = (piece == to_row(piece)) & (to_row(buckets) <= buckets)
    bias[...] = jnp.where(allowed, 0.0, NEG)
    arrived(recv_a, 3)
    qw[...] = unpack(recv_a[:, 0:half])
    kw[...] = unpack(recv_a[:, half : 2 * half])
    dw[...] = unpack(recv_a[:, 2 * half :])
    weights_into(win_p, qw, kw)
    attend_value_back(win_p, dw, out_m)
    send_d[...] = pack(out_m[...])
    exchange(send_d, recv_d, 16, 12, 13)

    arrived(recv_c, 11)
    vw[...] = unpack(recv_c[...])
    attend(win_p, vw, out_m)
    attend_back(win_p, qw, kw, vw, dw, out_q, out_k)
    send_r[:, 0:half] = pack(out_m[...])
    send_r[:, half : 2 * half] = pack(out_q[...])
    send_r[:, 2 * half :] = pack(out_k[...])
    exchange(send_r, recv_r, 16, 14, 15)

    def put_back(block):
        return dot(restore[...], unpack(block))

    arrived(recv_d, 13)
    grad_c[...] = put_back(recv_d[...]).astype(BF16)
    attend_value_back(stop_p, grad_c, grad_v)

    mine = (slice(None), pl.ds(pl.multiple_of(core * half, half), half))
    other = (slice(None), pl.ds(pl.multiple_of((1 - core) * half, half), half))
    rs0_send[...] = dot_tn(feat[...], grad_v[other]).astype(BF16)
    swap_0 = pltpu.make_async_remote_copy(
        src_ref=rs0_send, dst_ref=rs0_recv, send_sem=sems.at[16], recv_sem=sems.at[17],
        device_id=(grp, sibling), device_id_type=MESH,
    )
    swap_0.start()
    gw_own[...] = dot_tn(feat[...], grad_v[mine])
    swap_0.wait()
    rs1_send[...] = (gw_own[...] + rs0_recv[...].astype(F32)).astype(BF16).reshape(GROUPS, 64, half)
    rs1_recv[grp] = rs1_send[grp]

    @pl.loop(1, GROUPS)
    def _(step):
        peer = group(step)
        pltpu.make_async_remote_copy(
            src_ref=rs1_send.at[peer], dst_ref=rs1_recv.at[grp], send_sem=sems.at[18], recv_sem=sems.at[19],
            device_id=(peer, trn), device_id_type=MESH,
        ).start()

    attend_back(stop_p, query, key, vals, grad_c, stop_q, stop_k)

    wait_for(rs1_recv.at[pl.ds(0, GROUPS - 1)], 19)
    total = rs1_recv[0].astype(F32)
    for step in range(1, GROUPS):
        total = total + rs1_recv[step].astype(F32)
    for step in range(CHIPS):
        rs2_send[step] = total[4 * step : 4 * step + 4]
    rs2_recv[chip] = rs2_send[chip]

    @pl.loop(1, CHIPS)
    def _(step):
        peer = lax.rem(chip + step, CHIPS)
        pltpu.make_async_remote_copy(
            src_ref=rs2_send.at[peer], dst_ref=rs2_recv.at[chip], send_sem=sems.at[20], recv_sem=sems.at[21],
            device_id=(grp, peer * 2 + core), device_id_type=MESH,
        ).start()

    gfeat_o[...] = dot_nt(grad_v[...], w_full[...].reshape(D, HD)).astype(BF16)

    wait_for(rs2_recv.at[pl.ds(0, CHIPS - 1)], 21)
    mine_4 = rs2_recv[0]
    for step in range(1, CHIPS):
        mine_4 = mine_4 + rs2_recv[step]
    mine_4 = mine_4 * ((R * MEMBERS * GROUPS) ** -0.5)
    first, second = mine_4[0:2], mine_4[2:4]
    is_first = core == 0
    rs3_send[...] = jnp.where(is_first, second, first)
    swap_3 = pltpu.make_async_remote_copy(
        src_ref=rs3_send, dst_ref=rs3_recv, send_sem=sems.at[22], recv_sem=sems.at[23],
        device_id=(grp, sibling), device_id_type=MESH,
    )
    swap_3.start()
    kept = jnp.where(is_first, first, second)
    swap_3.wait()
    swapped = rs3_recv[...]
    gw_o[:, 0:half] = jnp.where(is_first, kept, swapped)
    gw_o[:, half:] = jnp.where(is_first, swapped, kept)

    arrived(recv_r, 15)
    mixed_o[...] = put_back(recv_r[:, 0:half]).astype(BF16)
    gq_o[...] = (stop_q[...] + put_back(recv_r[:, half : 2 * half])).astype(BF16)
    gk_o[...] = (stop_k[...] + put_back(recv_r[:, 2 * half :])).astype(BF16)

    sent(send_a, 16, 2)
    sent(send_m, 1, 4)
    sent(send_c, 16, 10)
    sent(send_d, 16, 12)
    sent(send_r, 16, 14)
    wait_for(w_recv.at[pl.ds(0, CHIPS - 1)], 0)

    @pl.when(jnp.logical_not(own_near))
    def _():
        wait_for(w_send, 0)

    wait_for(rs1_send.at[pl.ds(0, GROUPS - 1)], 18)
    wait_for(rs2_send.at[pl.ds(0, CHIPS - 1)], 20)


def shards(features, query_rows, key_rows, w_value, cotangent, station, bucket, slot_index):
    half = HD // 2
    vmem = pl.BlockSpec(memory_space=pltpu.VMEM)

    def buffer(shape, dtype):
        return pltpu.VMEM(shape, dtype)

    scratch = [
        buffer((R, R), BF16), buffer((R, R), BF16), buffer((R, R), F32),
        buffer((HEADS, R, R), BF16), buffer((HEADS, R, R), BF16),
        buffer((2 * R, 3 * half), BF16), buffer((2 * R, 3 * half), BF16),
        buffer((MEMBERS, 1, 128), I32), buffer((MEMBERS, 1, 128), I32),
        buffer((2 * R, half), BF16), buffer((2 * R, half), BF16),
        buffer((2 * R, half), BF16), buffer((2 * R, half), BF16),
        buffer((2 * R, 3 * half), BF16), buffer((2 * R, 3 * half), BF16),
        buffer((2, HD), F32), buffer((CHIPS, 2, HD), F32), buffer((32, HD), F32), buffer((GROUPS, 2, 32, HD), BF16),
        buffer((R, HD), BF16), buffer((R, HD), BF16), buffer((R, HD), BF16), buffer((R, HD), BF16),
        buffer((R, HD), F32), buffer((R, HD), F32),
        buffer((R, HD), BF16), buffer((R, HD), BF16), buffer((R, HD), BF16), buffer((R, HD), BF16),
        buffer((R, HD), F32), buffer((R, HD), F32), buffer((R, HD), F32),
        buffer((D, half), F32), buffer((D, half), BF16), buffer((D, half), BF16),
        buffer((GROUPS, 64, half), BF16), buffer((GROUPS, 64, half), BF16),
        buffer((CHIPS, 4, half), F32), buffer((CHIPS, 4, half), F32),
        buffer((2, half), F32), buffer((2, half), F32),
        pltpu.SemaphoreType.DMA((24,)),
    ]
    return pl.pallas_call(
        kernel,
        out_shape=(
            jax.ShapeDtypeStruct((R, HD), BF16),
            jax.ShapeDtypeStruct((R, D), BF16),
            jax.ShapeDtypeStruct((R, HD), BF16),
            jax.ShapeDtypeStruct((R, HD), BF16),
            jax.ShapeDtypeStruct((2, HD), F32),
        ),
        in_specs=[vmem] * 8,
        out_specs=(vmem,) * 5,
        scratch_shapes=scratch,
        compiler_params=pltpu.CompilerParams(
            collective_id=0, has_side_effects=True, vmem_limit_bytes=48 * 1024 * 1024
        ),
        name="delay_attention",
    )(
        features, query_rows, key_rows, w_value, cotangent,
        station.reshape(1, R), bucket.reshape(1, R), slot_index.reshape(1, R),
    )


def solution(mesh):
    rows = P(("grp", "trn"), None)
    ids = P(("grp", "trn"))
    return jax.shard_map(
        shards,
        mesh=mesh,
        in_specs=(rows,) * 5 + (ids,) * 3,
        out_specs=(rows,) * 5,
        check_vma=False,
    )
```

```python
import functools

import jax
import jax.numpy as jnp
from jax import lax
from jax.experimental import pallas as pl
from jax.experimental.pallas import tpu as pltpu
from jax.sharding import PartitionSpec as P

MESH = pl.DeviceIdType.MESH
BF16 = jnp.bfloat16
F32 = jnp.float32
I32 = jnp.int32
HEADS = 8
HDIM = 64
HD = 512
D = 1024
R = 256
WIN = 128
MEMBERS = 32
GROUPS = 16
CHIPS = 16
NEG = -1e30


def dot(a, b):
    return lax.dot_general(a, b, (((1,), (0,)), ((), ())), preferred_element_type=F32)


def dot_nt(a, b):
    return lax.dot_general(a, b, (((1,), (1,)), ((), ())), preferred_element_type=F32)


def dot_tn(a, b):
    return lax.dot_general(a, b, (((0,), (0,)), ((), ())), preferred_element_type=F32)


def iota(shape, dim):
    return lax.broadcasted_iota(I32, shape, dim)


def to_col(row):
    eye = iota((R, R), 0) == iota((R, R), 1)
    return jnp.sum(jnp.where(eye, jnp.broadcast_to(row, (R, R)), 0), axis=1, keepdims=True)


def to_row(col):
    eye = iota((R, R), 0) == iota((R, R), 1)
    return jnp.sum(jnp.where(eye, jnp.broadcast_to(col, (R, R)), 0), axis=0, keepdims=True)


def pack(rows):
    cut = rows.reshape(MEMBERS, 8, HD)
    return jnp.concatenate([cut[:, :, : HD // 2], cut[:, :, HD // 2 :]], axis=1).reshape(2 * R, HD // 2).astype(BF16)


def unpack(block):
    cut = block.astype(F32).reshape(MEMBERS, 16, HD // 2)
    low = cut[:, :8].reshape(R, HD // 2)
    high = cut[:, 8:].reshape(R, HD // 2)
    return jnp.concatenate([low, high], axis=1).astype(BF16)


def softmax(scores):
    top = jnp.max(scores, axis=1, keepdims=True)
    raised = jnp.exp(scores - top)
    return raised * (1.0 / jnp.sum(raised, axis=1, keepdims=True))


def kernel(
    feat_in, query_in, key_in, w_in, cot_in, station_in, bucket_in, slot_in,
    mixed_o, gfeat_o, gq_o, gk_o, gw_o,
    feat, query, key, w_part, cot, station, bucket, slot,
    order, restore, bias, stop_p, win_p,
    send, recv, send_m, recv_m,
    w_send, w_recv, w_rows, w_full,
    vals, ctx, grad_c, grad_v, stop_q, stop_k,
    qw, kw, vw, dw, out_m, out_q, out_k,
    gw_own, rs0_send, rs0_recv, rs1_send, rs1_recv, rs1_sum, rs2_swap, rs2_rows, rs2_send, rs2_recv,
    rs3_rows, rs3_send, rs3_recv,
    sems, in_sems, send_sems, recv_sems,
):
    copies_in = [
        pltpu.make_async_copy(source, target, in_sems.at[number])
        for number, (source, target) in enumerate((
            (slot_in, slot), (query_in, query), (w_in, w_part), (station_in, station), (bucket_in, bucket),
            (key_in, key), (cot_in, cot), (feat_in, feat),
        ))
    ]
    for copy in copies_in:
        copy.start()
    grp = lax.axis_index("grp")
    trn = lax.axis_index("trn")
    chip = trn // 2
    core = trn % 2
    sibling = chip * 2 + (1 - core)

    def member(step):
        return lax.rem(trn + step, MEMBERS)

    def group(step):
        return lax.rem(grp + step, GROUPS)

    barrier = pltpu.get_barrier_semaphore()

    @pl.loop(1, MEMBERS)
    def _(step):
        pl.semaphore_signal(barrier, inc=1, device_id=(grp, member(step)), device_id_type=MESH)

    @pl.loop(1, GROUPS)
    def _(step):
        pl.semaphore_signal(barrier, inc=1, device_id=(group(step), trn), device_id_type=MESH)

    def block(number, ref, who):
        return ref.at[number, pl.ds(pl.multiple_of(who * 16, 16), 16)]

    def exchange(number):
        pltpu.make_async_copy(block(number, send, trn), block(number, recv, trn), recv_sems.at[number]).start()

        @pl.loop(1, MEMBERS)
        def _(step):
            peer = member(step)
            pltpu.make_async_remote_copy(
                src_ref=block(number, send, peer), dst_ref=block(number, recv, trn),
                send_sem=send_sems.at[number], recv_sem=recv_sems.at[number],
                device_id=(grp, peer), device_id_type=MESH,
            ).start()

    def wait_for(ref, sem):
        pltpu.make_async_copy(ref, ref, sems.at[sem]).wait()

    def arrived(number):
        pltpu.make_async_copy(recv.at[number], recv.at[number], recv_sems.at[number]).wait()

    def sent(number):
        blocks = send.at[number, pl.ds(0, (MEMBERS - 1) * 16)]
        pltpu.make_async_copy(blocks, blocks, send_sems.at[number]).wait()

    copies_in[0].wait()
    slot_row = slot[...]
    goal_row = slot_row // R
    goal_col = to_col(goal_row)
    same = (goal_col == goal_row) & (iota((R, R), 0) < iota((R, R), 1))
    rank_row = jnp.sum(jnp.where(same, 1, 0), axis=0, keepdims=True)
    pos_row = goal_row * 8 + rank_row
    pos_col = to_col(pos_row)
    picks = iota((R, R), 0) == pos_row
    order[...] = jnp.where(picks, 1.0, 0.0).astype(BF16)

    half = HD // 2
    copies_in[1].wait()
    send[0] = pack(dot(order[...], query[...]))
    copies_in[2].wait()
    w_send[...] = w_part[...].astype(F32)

    pl.semaphore_wait(barrier, MEMBERS - 1 + GROUPS - 1)

    near = trn // 16
    index = lax.rem(trn, 16)
    own_near = core == near

    @pl.when(own_near)
    def _():
        pltpu.make_async_copy(w_send, w_recv.at[index], sems.at[1]).start()

    @pl.when(jnp.logical_not(own_near))
    def _():
        pltpu.make_async_remote_copy(
            src_ref=w_send, dst_ref=w_recv.at[index], send_sem=sems.at[0], recv_sem=sems.at[1],
            device_id=(grp, chip * 2 + near), device_id_type=MESH,
        ).start()

    @pl.loop(1, CHIPS)
    def _(step):
        pltpu.make_async_remote_copy(
            src_ref=w_send, dst_ref=w_recv.at[index], send_sem=sems.at[0], recv_sem=sems.at[1],
            device_id=(grp, lax.rem(chip + step, CHIPS) * 2 + near), device_id_type=MESH,
        ).start()

    exchange(0)
    copies_in[5].wait()
    send[1] = pack(dot(order[...], key[...]))
    exchange(1)

    copies_in[3].wait()
    copies_in[4].wait()
    lane = iota((R, 128), 1)
    within = iota((R, 128), 0) % 8

    def sorted_col(row):
        return jnp.sum(jnp.where(picks, jnp.broadcast_to(row, (R, R)), 0), axis=1, keepdims=True)

    place_col = sorted_col(slot_row % R)
    station_col = sorted_col(station[...])
    bucket_col = sorted_col(bucket[...])
    meta = (
        jnp.where(lane == within, place_col, 0)
        + jnp.where(lane == within + 8, station_col, 0)
        + jnp.where(lane == within + 16, bucket_col, 0)
    )
    send_m[...] = jnp.sum(meta.reshape(MEMBERS, 8, 128), axis=1, keepdims=True)

    def all_blocks_m(step):
        peer = member(step)
        pltpu.make_async_remote_copy(
            src_ref=send_m.at[peer], dst_ref=recv_m.at[trn], send_sem=sems.at[4], recv_sem=sems.at[5],
            device_id=(grp, peer), device_id_type=MESH,
        ).start()

    pltpu.make_async_copy(send_m.at[trn], recv_m.at[trn], sems.at[5]).start()
    pl.loop(1, MEMBERS)(all_blocks_m)

    copies_in[6].wait()
    send[2] = pack(dot(order[...], cot[...]))
    exchange(2)
    restore[...] = jnp.where(pos_col == iota((R, R), 1), 1.0, 0.0).astype(BF16)

    wait_for(w_recv, 1)
    for step in range(CHIPS):
        w_rows[2 * step : 2 * step + 2, :] = w_recv[step]
    w_full[grp, core] = w_rows[...].astype(BF16)

    @pl.loop(1, GROUPS)
    def _(step):
        pltpu.make_async_remote_copy(
            src_ref=w_full.at[grp, core], dst_ref=w_full.at[grp, core], send_sem=sems.at[6], recv_sem=sems.at[7],
            device_id=(group(step), trn), device_id_type=MESH,
        ).start()

    low_lane = iota((R, 128), 1) < HDIM

    def heads_of(ref, pair):
        part = ref[:, pl.ds(pl.multiple_of(pair * 128, 128), 128)]
        zero = jnp.zeros_like(part)
        return part, jnp.where(low_lane, part, zero), jnp.where(low_lane, zero, part)

    def cols(pair):
        return (slice(None), pl.ds(pl.multiple_of(pair * 128, 128), 128))

    def weights_into(target, q_ref, k_ref):
        @pl.loop(0, HEADS // 2)
        def _(pair):
            k_pair = k_ref[cols(pair)]
            _, *q_heads = heads_of(q_ref, pair)
            for head in range(2):
                scores = dot_nt(q_heads[head], k_pair) * (HDIM ** -0.5) + bias[...]
                target[2 * pair + head] = softmax(scores).astype(BF16)

    bias[...] = jnp.where(iota((R, R), 1) <= iota((R, R), 0), 0.0, NEG)
    weights_into(stop_p, query, key)

    wait_for(w_full.at[pl.ds(0, GROUPS - 1), core], 7)
    wait_for(w_full.at[pl.ds(0, GROUPS - 1), core], 6)
    swap_w = pltpu.make_async_remote_copy(
        src_ref=w_full.at[:, core], dst_ref=w_full.at[:, core], send_sem=sems.at[8], recv_sem=sems.at[9],
        device_id=(grp, sibling), device_id_type=MESH,
    )
    swap_w.start()
    swap_w.wait()

    weight = w_full[...].reshape(D, HD)
    copies_in[7].wait()
    vals[...] = dot(feat[...], weight).astype(BF16)

    def attend(p_ref, v_ref, out_ref):
        @pl.loop(0, HEADS // 2)
        def _(pair):
            v_pair = v_ref[cols(pair)]
            first = dot(p_ref[2 * pair], v_pair)
            second = dot(p_ref[2 * pair + 1], v_pair)
            out_ref[cols(pair)] = jnp.where(low_lane, first, second).astype(out_ref.dtype)

    def attend_value_back(p_ref, d_ref, out_ref):
        @pl.loop(0, HEADS // 2)
        def _(pair):
            d_pair = d_ref[cols(pair)]
            first = dot_tn(p_ref[2 * pair], d_pair)
            second = dot_tn(p_ref[2 * pair + 1], d_pair)
            out_ref[cols(pair)] = jnp.where(low_lane, first, second).astype(out_ref.dtype)

    def attend_back(p_ref, q_ref, k_ref, v_ref, d_ref, dq_ref, dk_ref):
        @pl.loop(0, HEADS // 2)
        def _(pair):
            q_pair, k_pair, v_pair = q_ref[cols(pair)], k_ref[cols(pair)], v_ref[cols(pair)]
            _, *d_heads = heads_of(d_ref, pair)
            dq, dk = [], []
            for head in range(2):
                weights = p_ref[2 * pair + head].astype(F32)
                grad = dot_nt(d_heads[head], v_pair)
                row_dot = jnp.sum(weights * grad, axis=1, keepdims=True)
                grad = (weights * (grad - row_dot)).astype(BF16)
                dq.append(dot(grad, k_pair))
                dk.append(dot_tn(grad, q_pair))
            factor = HDIM ** -0.5
            dq_ref[cols(pair)] = (jnp.where(low_lane, dq[0], dq[1]) * factor).astype(dq_ref.dtype)
            dk_ref[cols(pair)] = (jnp.where(low_lane, dk[0], dk[1]) * factor).astype(dk_ref.dtype)

    attend(stop_p, vals, ctx)
    send[3] = pack(dot(order[...], ctx[...]))
    exchange(3)

    wait_for(recv_m, 5)
    got = jnp.broadcast_to(recv_m[...], (MEMBERS, 8, 128)).reshape(R, 128)

    def field(number):
        return jnp.sum(jnp.where(lane == within + 8 * number, got, 0), axis=1, keepdims=True)

    piece = field(1) * 2 + field(0) // WIN
    buckets = field(2)
    allowed = (piece == to_row(piece)) & (to_row(buckets) <= buckets)
    bias[...] = jnp.where(allowed, 0.0, NEG)
    arrived(0)
    qw[...] = unpack(recv[0])
    arrived(1)
    kw[...] = unpack(recv[1])
    weights_into(win_p, qw, kw)
    arrived(2)
    dw[...] = unpack(recv[2])
    attend_value_back(win_p, dw, out_m)
    send[4] = pack(out_m[...])
    exchange(4)

    arrived(3)
    vw[...] = unpack(recv[3])
    attend(win_p, vw, out_m)
    send[5] = pack(out_m[...])
    exchange(5)
    attend_back(win_p, qw, kw, vw, dw, out_q, out_k)
    send[6] = pack(out_q[...])
    exchange(6)
    send[7] = pack(out_k[...])
    exchange(7)

    def put_back(number):
        arrived(number)
        return dot(restore[...], unpack(recv[number]))

    grad_c[...] = put_back(4).astype(BF16)
    attend_value_back(stop_p, grad_c, grad_v)

    mine = (slice(None), pl.ds(pl.multiple_of(core * half, half), half))
    other = (slice(None), pl.ds(pl.multiple_of((1 - core) * half, half), half))
    rs0_send[...] = dot_tn(feat[...], grad_v[other]).astype(BF16)
    swap_0 = pltpu.make_async_remote_copy(
        src_ref=rs0_send, dst_ref=rs0_recv, send_sem=sems.at[16], recv_sem=sems.at[17],
        device_id=(grp, sibling), device_id_type=MESH,
    )
    swap_0.start()
    gw_own[...] = dot_tn(feat[...], grad_v[mine])
    swap_0.wait()
    rs1_send[...] = (gw_own[...] + rs0_recv[...].astype(F32)).astype(BF16).reshape(GROUPS, 64, half)
    rs1_recv[grp] = rs1_send[grp]

    @pl.loop(1, GROUPS)
    def _(step):
        peer = group(step)
        pltpu.make_async_remote_copy(
            src_ref=rs1_send.at[peer], dst_ref=rs1_recv.at[grp], send_sem=sems.at[18], recv_sem=sems.at[19],
            device_id=(peer, trn), device_id_type=MESH,
        ).start()

    attend_back(stop_p, query, key, vals, grad_c, stop_q, stop_k)

    wait_for(rs1_recv.at[pl.ds(0, GROUPS - 1)], 19)
    total = rs1_recv[0].astype(F32)
    for step in range(1, GROUPS):
        total = total + rs1_recv[step].astype(F32)
    rs1_sum[...] = total

    swap_2 = pltpu.make_async_remote_copy(
        src_ref=rs1_sum.at[pl.ds(pl.multiple_of(32 * (1 - core), 32), 32)], dst_ref=rs2_swap,
        send_sem=sems.at[20], recv_sem=sems.at[21], device_id=(grp, sibling), device_id_type=MESH,
    )
    swap_2.start()
    gfeat_o[...] = dot_nt(grad_v[...], w_full[...].reshape(D, HD)).astype(BF16)
    swap_2.wait()
    is_first = core == 0
    kept = rs1_sum[pl.ds(pl.multiple_of(32 * core, 32), 32), :]
    swapped = rs2_swap[...]
    sides = (jnp.where(is_first, kept, swapped), jnp.where(is_first, swapped, kept))
    for step in range(CHIPS // 2):
        for part in range(4):
            piece_4 = sides[part // 2][4 * step : 4 * step + 4, 128 * (part % 2) : 128 * (part % 2) + 128]
            rs2_rows[16 * step + 4 * part : 16 * step + 4 * part + 4, :] = piece_4
    rs2_send[...] = rs2_rows[...].astype(BF16)

    def part_16(ref, who):
        return ref.at[pl.ds(pl.multiple_of(who * 16, 16), 16)]

    eight = lax.rem(chip, 8)
    summing = core == chip // 8

    @pl.when(summing)
    def _():
        pltpu.make_async_copy(part_16(rs2_send, eight), part_16(rs2_recv, chip), sems.at[23]).start()

    @pl.when(jnp.logical_not(summing))
    def _():
        pltpu.make_async_remote_copy(
            src_ref=part_16(rs2_send, eight), dst_ref=part_16(rs2_recv, chip),
            send_sem=sems.at[22], recv_sem=sems.at[23],
            device_id=(grp, (8 * core + eight) * 2 + core), device_id_type=MESH,
        ).start()

    @pl.loop(1, 8)
    def _(step):
        peer = lax.rem(eight + step, 8)
        pltpu.make_async_remote_copy(
            src_ref=part_16(rs2_send, peer), dst_ref=part_16(rs2_recv, chip),
            send_sem=sems.at[22], recv_sem=sems.at[23],
            device_id=(grp, (8 * core + peer) * 2 + core), device_id_type=MESH,
        ).start()

    mixed_o[...] = put_back(5).astype(BF16)
    gq_o[...] = (stop_q[...] + put_back(6)).astype(BF16)

    give = pltpu.make_async_remote_copy(
        src_ref=rs3_send, dst_ref=rs3_recv, send_sem=sems.at[2], recv_sem=sems.at[3],
        device_id=(grp, sibling), device_id_type=MESH,
    )

    @pl.when(summing)
    def _():
        wait_for(rs2_recv, 23)
        rows_16 = jnp.sum(rs2_recv[...].astype(F32).reshape(CHIPS, 16, 128), axis=0)
        rs3_rows[...] = rows_16 * ((R * MEMBERS * GROUPS) ** -0.5)
        four = [rs3_rows[4 * part : 4 * part + 4, :] for part in range(4)]
        rows_4 = jnp.concatenate(four, axis=1)
        rs3_send[...] = jnp.where(is_first, rows_4[2:4], rows_4[0:2])
        give.start()
        gw_o[...] = jnp.where(is_first, rows_4[0:2], rows_4[2:4])

    gk_o[...] = (stop_k[...] + put_back(7)).astype(BF16)

    @pl.when(summing)
    def _():
        give.wait_send()

    @pl.when(jnp.logical_not(summing))
    def _():
        give.wait_recv()
        gw_o[...] = rs3_recv[...]

    for number in range(8):
        sent(number)
    wait_for(send_m.at[pl.ds(0, MEMBERS - 1)], 4)
    wait_for(w_recv.at[pl.ds(0, CHIPS - 1)], 0)

    @pl.when(jnp.logical_not(own_near))
    def _():
        wait_for(w_send, 0)

    wait_for(rs1_send.at[pl.ds(0, GROUPS - 1)], 18)
    wait_for(rs2_send.at[pl.ds(0, 7 * 16)], 22)

    @pl.when(jnp.logical_not(summing))
    def _():
        wait_for(rs2_send.at[pl.ds(0, 16)], 22)


def write(*refs):
    *pairs, sems = refs
    copies = [
        pltpu.make_async_copy(source, target, sems.at[number])
        for number, (source, target) in enumerate(zip(pairs[:5], pairs[5:]))
    ]
    for copy in copies:
        copy.start()
    for copy in copies:
        copy.wait()


def shards(features, query_rows, key_rows, w_value, cotangent, station, bucket, slot_index):
    half = HD // 2
    vmem = pl.BlockSpec(memory_space=pltpu.VMEM)

    def buffer(shape, dtype):
        return pltpu.VMEM(shape, dtype)

    scratch = [
        buffer((R, D), BF16), buffer((R, HD), BF16), buffer((R, HD), BF16), buffer((2, HD), BF16), buffer((R, HD), BF16),
        buffer((1, R), I32), buffer((1, R), I32), buffer((1, R), I32),
        buffer((R, R), BF16), buffer((R, R), BF16), buffer((R, R), F32),
        buffer((HEADS, R, R), BF16), buffer((HEADS, R, R), BF16),
        buffer((8, 2 * R, half), BF16), buffer((8, 2 * R, half), BF16),
        buffer((MEMBERS, 1, 128), I32), buffer((MEMBERS, 1, 128), I32),
        buffer((2, HD), F32), buffer((CHIPS, 2, HD), F32), buffer((32, HD), F32), buffer((GROUPS, 2, 32, HD), BF16),
        buffer((R, HD), BF16), buffer((R, HD), BF16), buffer((R, HD), BF16), buffer((R, HD), BF16),
        buffer((R, HD), F32), buffer((R, HD), F32),
        buffer((R, HD), BF16), buffer((R, HD), BF16), buffer((R, HD), BF16), buffer((R, HD), BF16),
        buffer((R, HD), F32), buffer((R, HD), F32), buffer((R, HD), F32),
        buffer((D, half), F32), buffer((D, half), BF16), buffer((D, half), BF16),
        buffer((GROUPS, 64, half), BF16), buffer((GROUPS, 64, half), BF16),
        buffer((64, half), F32), buffer((32, half), F32), buffer((128, 128), F32), buffer((128, 128), BF16),
        buffer((R, 128), BF16), buffer((16, 128), F32), buffer((2, HD), F32), buffer((2, HD), F32),
        pltpu.SemaphoreType.DMA((24,)), pltpu.SemaphoreType.DMA((8,)),
        pltpu.SemaphoreType.DMA((8,)), pltpu.SemaphoreType.DMA((8,)),
    ]
    kinds = (((R, HD), BF16), ((R, D), BF16), ((R, HD), BF16), ((R, HD), BF16), ((2, HD), F32))
    inputs = (
        features, query_rows, key_rows, w_value, cotangent,
        station.reshape(1, R), bucket.reshape(1, R), slot_index.reshape(1, R),
    )
    results = pl.pallas_call(
        kernel,
        out_shape=tuple(pltpu.VMEM(*kind) for kind in kinds),
        in_specs=[pl.BlockSpec(memory_space=pltpu.HBM)] * 8,
        out_specs=(vmem,) * 5,
        scratch_shapes=scratch,
        compiler_params=pltpu.CompilerParams(
            collective_id=0, has_side_effects=True, vmem_limit_bytes=48 * 1024 * 1024
        ),
        name="delay_attention",
    )(*(pltpu.with_memory_space_constraint(array, pltpu.HBM) for array in inputs))
    return pl.pallas_call(
        write,
        out_shape=tuple(jax.ShapeDtypeStruct(*kind) for kind in kinds),
        in_specs=[vmem] * 5,
        out_specs=(pl.BlockSpec(memory_space=pltpu.HBM),) * 5,
        scratch_shapes=[pltpu.SemaphoreType.DMA((5,))],
        name="write_results",
    )(*(pltpu.with_memory_space_constraint(array, pltpu.VMEM) for array in results))


def solution(mesh):
    rows = P(("grp", "trn"), None)
    ids = P(("grp", "trn"))
    return jax.shard_map(
        shards,
        mesh=mesh,
        in_specs=(rows,) * 5 + (ids,) * 3,
        out_specs=(rows,) * 5,
        check_vma=False,
    )
```

```python
import functools

import jax
import jax.numpy as jnp
from jax import lax
from jax.experimental import pallas as pl
from jax.experimental.pallas import tpu as pltpu
from jax.sharding import PartitionSpec as P

MESH = pl.DeviceIdType.MESH
BF16 = jnp.bfloat16
F32 = jnp.float32
I32 = jnp.int32
HEADS = 8
HDIM = 64
HD = 512
D = 1024
R = 256
WIN = 128
MEMBERS = 32
GROUPS = 16
CHIPS = 16
NEG = -1e30


def dot(a, b):
    return lax.dot_general(a, b, (((1,), (0,)), ((), ())), preferred_element_type=F32)


def dot_nt(a, b):
    return lax.dot_general(a, b, (((1,), (1,)), ((), ())), preferred_element_type=F32)


def dot_tn(a, b):
    return lax.dot_general(a, b, (((0,), (0,)), ((), ())), preferred_element_type=F32)


def iota(shape, dim):
    return lax.broadcasted_iota(I32, shape, dim)


def to_col(row):
    eye = iota((R, R), 0) == iota((R, R), 1)
    return jnp.sum(jnp.where(eye, jnp.broadcast_to(row, (R, R)), 0), axis=1, keepdims=True)


def to_row(col):
    eye = iota((R, R), 0) == iota((R, R), 1)
    return jnp.sum(jnp.where(eye, jnp.broadcast_to(col, (R, R)), 0), axis=0, keepdims=True)


def pack(rows):
    cut = rows.reshape(MEMBERS, 8, HD)
    return jnp.concatenate([cut[:, :, : HD // 2], cut[:, :, HD // 2 :]], axis=1).reshape(2 * R, HD // 2).astype(BF16)


def unpack(block):
    cut = block.astype(F32).reshape(MEMBERS, 16, HD // 2)
    low = cut[:, :8].reshape(R, HD // 2)
    high = cut[:, 8:].reshape(R, HD // 2)
    return jnp.concatenate([low, high], axis=1).astype(BF16)


def softmax(scores):
    top = jnp.max(scores, axis=1, keepdims=True)
    raised = jnp.exp(scores - top)
    return raised * (1.0 / jnp.sum(raised, axis=1, keepdims=True))


def kernel(
    feat_in, query_in, key_in, w_in, cot_in, station_in, bucket_in, slot_in,
    mixed_o, gfeat_o, gq_o, gk_o, gw_o,
    feat, query, key, w_part, cot, station, bucket, slot,
    order, restore, bias, stop_p, win_p,
    send, recv, send_m, recv_m,
    w_pair, w_block, w_send, w_recv, w_rows, w_full,
    vals, ctx, grad_c, grad_v, stop_q, stop_k,
    qw, kw, vw, dw, out_m, out_q, out_k,
    gw_own, rs0_send, rs0_recv, rs1_send, rs1_recv, rs1_sum, rs2_swap, rs2_rows, rs2_send, rs2_recv,
    rs3_rows, rs3_send, rs3_recv,
    sems, in_sems, send_sems, recv_sems,
):
    copies_in = [
        pltpu.make_async_copy(source, target, in_sems.at[number])
        for number, (source, target) in enumerate((
            (slot_in, slot), (query_in, query), (w_in, w_part), (station_in, station), (bucket_in, bucket),
            (key_in, key), (cot_in, cot), (feat_in, feat),
        ))
    ]
    for copy in copies_in:
        copy.start()
    grp = lax.axis_index("grp")
    trn = lax.axis_index("trn")
    chip = trn // 2
    core = trn % 2
    sibling = chip * 2 + (1 - core)

    def member(step):
        return lax.rem(trn + step, MEMBERS)

    def group(step):
        return lax.rem(grp + step, GROUPS)

    barrier = pltpu.get_barrier_semaphore()

    @pl.loop(1, MEMBERS)
    def _(step):
        pl.semaphore_signal(barrier, inc=1, device_id=(grp, member(step)), device_id_type=MESH)

    @pl.loop(1, GROUPS)
    def _(step):
        pl.semaphore_signal(barrier, inc=1, device_id=(group(step), trn), device_id_type=MESH)

    def block(number, ref, who):
        return ref.at[number, pl.ds(pl.multiple_of(who * 16, 16), 16)]

    def exchange(number, first=1, last=MEMBERS):
        if first == 1:
            pltpu.make_async_copy(block(number, send, trn), block(number, recv, trn), recv_sems.at[number]).start()

        @pl.loop(first, last)
        def _(step):
            peer = member(step)
            pltpu.make_async_remote_copy(
                src_ref=block(number, send, peer), dst_ref=block(number, recv, trn),
                send_sem=send_sems.at[number], recv_sem=recv_sems.at[number],
                device_id=(grp, peer), device_id_type=MESH,
            ).start()

    def wait_for(ref, sem):
        pltpu.make_async_copy(ref, ref, sems.at[sem]).wait()

    def arrived(number):
        pltpu.make_async_copy(recv.at[number], recv.at[number], recv_sems.at[number]).wait()

    def sent(number):
        blocks = send.at[number, pl.ds(0, (MEMBERS - 1) * 16)]
        pltpu.make_async_copy(blocks, blocks, send_sems.at[number]).wait()

    copies_in[0].wait()
    slot_row = slot[...]
    goal_row = slot_row // R
    goal_col = to_col(goal_row)
    same = (goal_col == goal_row) & (iota((R, R), 0) < iota((R, R), 1))
    rank_row = jnp.sum(jnp.where(same, 1, 0), axis=0, keepdims=True)
    pos_row = goal_row * 8 + rank_row
    pos_col = to_col(pos_row)
    picks = iota((R, R), 0) == pos_row
    order[...] = jnp.where(picks, 1.0, 0.0).astype(BF16)

    half = HD // 2
    copies_in[1].wait()
    send[0] = pack(dot(order[...], query[...]))
    copies_in[2].wait()
    w_pair[core] = w_part[...].astype(F32)

    pl.semaphore_wait(barrier, MEMBERS - 1 + GROUPS - 1)

    share = pltpu.make_async_remote_copy(
        src_ref=w_pair.at[core], dst_ref=w_pair.at[core], send_sem=sems.at[0], recv_sem=sems.at[1],
        device_id=(grp, sibling), device_id_type=MESH,
    )
    share.start()
    exchange(0, 1, 9)
    share.wait()
    four_rows = w_pair[...].reshape(4, HD)
    for part in range(4):
        w_block[4 * part : 4 * part + 4, :] = four_rows[:, 128 * part : 128 * part + 128]
    w_send[...] = w_block[...].astype(BF16)
    near = chip // 8
    eight = lax.rem(chip, 8)

    def part_16(ref, who):
        return ref.at[pl.ds(pl.multiple_of(who * 16, 16), 16)]

    @pl.when(core == near)
    def _():
        pltpu.make_async_copy(w_send, part_16(w_recv, eight), sems.at[9]).start()

    def send_weights(away):
        pltpu.make_async_remote_copy(
            src_ref=w_send, dst_ref=part_16(w_recv, eight), send_sem=sems.at[8], recv_sem=sems.at[9],
            device_id=(grp, lax.rem(chip + CHIPS + away, CHIPS) * 2 + near), device_id_type=MESH,
        ).start()

    pl.loop(1, 8)(lambda step: send_weights(step * (1 - 2 * core)))

    @pl.when(core == 0)
    def _():
        send_weights(8)

    exchange(0, 9)
    copies_in[5].wait()
    send[1] = pack(dot(order[...], key[...]))
    exchange(1)

    copies_in[3].wait()
    copies_in[4].wait()
    lane = iota((R, 128), 1)
    within = iota((R, 128), 0) % 8

    def sorted_col(row):
        return jnp.sum(jnp.where(picks, jnp.broadcast_to(row, (R, R)), 0), axis=1, keepdims=True)

    place_col = sorted_col(slot_row % R)
    station_col = sorted_col(station[...])
    bucket_col = sorted_col(bucket[...])
    meta = (
        jnp.where(lane == within, place_col, 0)
        + jnp.where(lane == within + 8, station_col, 0)
        + jnp.where(lane == within + 16, bucket_col, 0)
    )
    send_m[...] = jnp.sum(meta.reshape(MEMBERS, 8, 128), axis=1, keepdims=True)

    def all_blocks_m(step):
        peer = member(step)
        pltpu.make_async_remote_copy(
            src_ref=send_m.at[peer], dst_ref=recv_m.at[trn], send_sem=sems.at[4], recv_sem=sems.at[5],
            device_id=(grp, peer), device_id_type=MESH,
        ).start()

    pltpu.make_async_copy(send_m.at[trn], recv_m.at[trn], sems.at[5]).start()
    pl.loop(1, MEMBERS)(all_blocks_m)

    copies_in[6].wait()
    send[2] = pack(dot(order[...], cot[...]))
    exchange(2)
    restore[...] = jnp.where(pos_col == iota((R, R), 1), 1.0, 0.0).astype(BF16)

    wait_for(w_recv, 9)
    wide = w_recv[...].astype(F32)
    for step in range(8):
        for part in range(4):
            first_row = 16 * step + 4 * part
            w_rows[4 * step : 4 * step + 4, 128 * part : 128 * part + 128] = wide[first_row : first_row + 4]
    w_full[grp, core] = w_rows[...].astype(BF16)

    @pl.loop(1, GROUPS)
    def _(step):
        pltpu.make_async_remote_copy(
            src_ref=w_full.at[grp, core], dst_ref=w_full.at[grp, core], send_sem=sems.at[6], recv_sem=sems.at[7],
            device_id=(group(step), trn), device_id_type=MESH,
        ).start()

    low_lane = iota((R, 128), 1) < HDIM

    def heads_of(ref, pair):
        part = ref[:, pl.ds(pl.multiple_of(pair * 128, 128), 128)]
        zero = jnp.zeros_like(part)
        return part, jnp.where(low_lane, part, zero), jnp.where(low_lane, zero, part)

    def cols(pair):
        return (slice(None), pl.ds(pl.multiple_of(pair * 128, 128), 128))

    def weights_into(target, q_ref, k_ref):
        @pl.loop(0, HEADS // 2)
        def _(pair):
            k_pair = k_ref[cols(pair)]
            _, *q_heads = heads_of(q_ref, pair)
            for head in range(2):
                scores = dot_nt(q_heads[head], k_pair) * (HDIM ** -0.5) + bias[...]
                target[2 * pair + head] = softmax(scores).astype(BF16)

    bias[...] = jnp.where(iota((R, R), 1) <= iota((R, R), 0), 0.0, NEG)
    weights_into(stop_p, query, key)

    wait_for(w_full.at[pl.ds(0, GROUPS - 1), core], 7)
    wait_for(w_full.at[pl.ds(0, GROUPS - 1), core], 6)
    swap_w = pltpu.make_async_remote_copy(
        src_ref=w_full.at[:, core], dst_ref=w_full.at[:, core], send_sem=sems.at[10], recv_sem=sems.at[11],
        device_id=(grp, sibling), device_id_type=MESH,
    )
    swap_w.start()
    swap_w.wait()

    weight = w_full[...].reshape(D, HD)
    copies_in[7].wait()
    vals[...] = dot(feat[...], weight).astype(BF16)

    def attend(p_ref, v_ref, out_ref):
        @pl.loop(0, HEADS // 2)
        def _(pair):
            v_pair = v_ref[cols(pair)]
            first = dot(p_ref[2 * pair], v_pair)
            second = dot(p_ref[2 * pair + 1], v_pair)
            out_ref[cols(pair)] = jnp.where(low_lane, first, second).astype(out_ref.dtype)

    def attend_value_back(p_ref, d_ref, out_ref):
        @pl.loop(0, HEADS // 2)
        def _(pair):
            d_pair = d_ref[cols(pair)]
            first = dot_tn(p_ref[2 * pair], d_pair)
            second = dot_tn(p_ref[2 * pair + 1], d_pair)
            out_ref[cols(pair)] = jnp.where(low_lane, first, second).astype(out_ref.dtype)

    def attend_back(p_ref, q_ref, k_ref, v_ref, d_ref, dq_ref, dk_ref):
        @pl.loop(0, HEADS // 2)
        def _(pair):
            q_pair, k_pair, v_pair = q_ref[cols(pair)], k_ref[cols(pair)], v_ref[cols(pair)]
            _, *d_heads = heads_of(d_ref, pair)
            dq, dk = [], []
            for head in range(2):
                weights = p_ref[2 * pair + head].astype(F32)
                grad = dot_nt(d_heads[head], v_pair)
                row_dot = jnp.sum(weights * grad, axis=1, keepdims=True)
                grad = (weights * (grad - row_dot)).astype(BF16)
                dq.append(dot(grad, k_pair))
                dk.append(dot_tn(grad, q_pair))
            factor = HDIM ** -0.5
            dq_ref[cols(pair)] = (jnp.where(low_lane, dq[0], dq[1]) * factor).astype(dq_ref.dtype)
            dk_ref[cols(pair)] = (jnp.where(low_lane, dk[0], dk[1]) * factor).astype(dk_ref.dtype)

    attend(stop_p, vals, ctx)
    send[3] = pack(dot(order[...], ctx[...]))
    exchange(3)

    wait_for(recv_m, 5)
    got = jnp.broadcast_to(recv_m[...], (MEMBERS, 8, 128)).reshape(R, 128)

    def field(number):
        return jnp.sum(jnp.where(lane == within + 8 * number, got, 0), axis=1, keepdims=True)

    piece = field(1) * 2 + field(0) // WIN
    buckets = field(2)
    allowed = (piece == to_row(piece)) & (to_row(buckets) <= buckets)
    bias[...] = jnp.where(allowed, 0.0, NEG)
    arrived(0)
    qw[...] = unpack(recv[0])
    arrived(1)
    kw[...] = unpack(recv[1])
    weights_into(win_p, qw, kw)
    arrived(2)
    dw[...] = unpack(recv[2])
    attend_value_back(win_p, dw, out_m)
    send[4] = pack(out_m[...])
    exchange(4)

    arrived(3)
    vw[...] = unpack(recv[3])
    attend(win_p, vw, out_m)
    send[5] = pack(out_m[...])
    exchange(5)
    attend_back(win_p, qw, kw, vw, dw, out_q, out_k)
    send[6] = pack(out_q[...])
    exchange(6)
    send[7] = pack(out_k[...])

    def put_back(number):
        arrived(number)
        return dot(restore[...], unpack(recv[number]))

    grad_c[...] = put_back(4).astype(BF16)
    attend_value_back(stop_p, grad_c, grad_v)

    mine = (slice(None), pl.ds(pl.multiple_of(core * half, half), half))
    other = (slice(None), pl.ds(pl.multiple_of((1 - core) * half, half), half))
    rs0_send[...] = dot_tn(feat[...], grad_v[other]).astype(BF16)
    swap_0 = pltpu.make_async_remote_copy(
        src_ref=rs0_send, dst_ref=rs0_recv, send_sem=sems.at[16], recv_sem=sems.at[17],
        device_id=(grp, sibling), device_id_type=MESH,
    )
    swap_0.start()
    gw_own[...] = dot_tn(feat[...], grad_v[mine])
    swap_0.wait()
    rs1_send[...] = (gw_own[...] + rs0_recv[...].astype(F32)).astype(BF16).reshape(GROUPS, 64, half)
    rs1_recv[grp] = rs1_send[grp]

    @pl.loop(1, GROUPS)
    def _(step):
        peer = group(step)
        pltpu.make_async_remote_copy(
            src_ref=rs1_send.at[peer], dst_ref=rs1_recv.at[grp], send_sem=sems.at[18], recv_sem=sems.at[19],
            device_id=(peer, trn), device_id_type=MESH,
        ).start()

    attend_back(stop_p, query, key, vals, grad_c, stop_q, stop_k)

    wait_for(rs1_recv.at[pl.ds(0, GROUPS - 1)], 19)
    total = rs1_recv[0].astype(F32)
    for step in range(1, GROUPS):
        total = total + rs1_recv[step].astype(F32)
    rs1_sum[...] = total

    swap_2 = pltpu.make_async_remote_copy(
        src_ref=rs1_sum.at[pl.ds(pl.multiple_of(32 * (1 - core), 32), 32)], dst_ref=rs2_swap,
        send_sem=sems.at[20], recv_sem=sems.at[21], device_id=(grp, sibling), device_id_type=MESH,
    )
    swap_2.start()
    gfeat_o[...] = dot_nt(grad_v[...], w_full[...].reshape(D, HD)).astype(BF16)
    swap_2.wait()
    is_first = core == 0
    kept = rs1_sum[pl.ds(pl.multiple_of(32 * core, 32), 32), :]
    swapped = rs2_swap[...]
    sides = (jnp.where(is_first, kept, swapped), jnp.where(is_first, swapped, kept))
    for step in range(CHIPS // 2):
        for part in range(4):
            piece_4 = sides[part // 2][4 * step : 4 * step + 4, 128 * (part % 2) : 128 * (part % 2) + 128]
            rs2_rows[16 * step + 4 * part : 16 * step + 4 * part + 4, :] = piece_4
    rs2_send[...] = rs2_rows[...].astype(BF16)

    summing = core == near

    @pl.when(summing)
    def _():
        pltpu.make_async_copy(part_16(rs2_send, eight), part_16(rs2_recv, chip), sems.at[23]).start()

    @pl.when(jnp.logical_not(summing))
    def _():
        pltpu.make_async_remote_copy(
            src_ref=part_16(rs2_send, eight), dst_ref=part_16(rs2_recv, chip),
            send_sem=sems.at[22], recv_sem=sems.at[23],
            device_id=(grp, (8 * core + eight) * 2 + core), device_id_type=MESH,
        ).start()

    @pl.loop(1, 8)
    def _(step):
        peer = lax.rem(eight + step, 8)
        pltpu.make_async_remote_copy(
            src_ref=part_16(rs2_send, peer), dst_ref=part_16(rs2_recv, chip),
            send_sem=sems.at[22], recv_sem=sems.at[23],
            device_id=(grp, (8 * core + peer) * 2 + core), device_id_type=MESH,
        ).start()

    exchange(7)

    mixed_o[...] = put_back(5).astype(BF16)
    gq_o[...] = (stop_q[...] + put_back(6)).astype(BF16)

    give = pltpu.make_async_remote_copy(
        src_ref=rs3_send, dst_ref=rs3_recv, send_sem=sems.at[2], recv_sem=sems.at[3],
        device_id=(grp, sibling), device_id_type=MESH,
    )

    @pl.when(summing)
    def _():
        wait_for(rs2_recv, 23)
        rows_16 = jnp.sum(rs2_recv[...].astype(F32).reshape(CHIPS, 16, 128), axis=0)
        rs3_rows[...] = rows_16 * ((R * MEMBERS * GROUPS) ** -0.5)
        four = [rs3_rows[4 * part : 4 * part + 4, :] for part in range(4)]
        rows_4 = jnp.concatenate(four, axis=1)
        rs3_send[...] = jnp.where(is_first, rows_4[2:4], rows_4[0:2])
        give.start()
        gw_o[...] = jnp.where(is_first, rows_4[0:2], rows_4[2:4])

    gk_o[...] = (stop_k[...] + put_back(7)).astype(BF16)

    @pl.when(summing)
    def _():
        give.wait_send()

    @pl.when(jnp.logical_not(summing))
    def _():
        give.wait_recv()
        gw_o[...] = rs3_recv[...]

    for number in range(8):
        sent(number)
    wait_for(send_m.at[pl.ds(0, MEMBERS - 1)], 4)
    wait_for(w_recv.at[pl.ds(0, 7 * 16)], 8)

    @pl.when(core == 0)
    def _():
        wait_for(w_send, 8)

    wait_for(rs1_send.at[pl.ds(0, GROUPS - 1)], 18)
    wait_for(rs2_send.at[pl.ds(0, 7 * 16)], 22)

    @pl.when(jnp.logical_not(summing))
    def _():
        wait_for(rs2_send.at[pl.ds(0, 16)], 22)


def write(*refs):
    *pairs, sems = refs
    copies = [
        pltpu.make_async_copy(source, target, sems.at[number])
        for number, (source, target) in enumerate(zip(pairs[:5], pairs[5:]))
    ]
    for copy in copies:
        copy.start()
    for copy in copies:
        copy.wait()


def shards(features, query_rows, key_rows, w_value, cotangent, station, bucket, slot_index):
    half = HD // 2
    vmem = pl.BlockSpec(memory_space=pltpu.VMEM)

    def buffer(shape, dtype):
        return pltpu.VMEM(shape, dtype)

    scratch = [
        buffer((R, D), BF16), buffer((R, HD), BF16), buffer((R, HD), BF16), buffer((2, HD), BF16), buffer((R, HD), BF16),
        buffer((1, R), I32), buffer((1, R), I32), buffer((1, R), I32),
        buffer((R, R), BF16), buffer((R, R), BF16), buffer((R, R), F32),
        buffer((HEADS, R, R), BF16), buffer((HEADS, R, R), BF16),
        buffer((8, 2 * R, half), BF16), buffer((8, 2 * R, half), BF16),
        buffer((MEMBERS, 1, 128), I32), buffer((MEMBERS, 1, 128), I32),
        buffer((2, 2, HD), F32), buffer((16, 128), F32), buffer((16, 128), BF16), buffer((128, 128), BF16),
        buffer((32, HD), F32), buffer((GROUPS, 2, 32, HD), BF16),
        buffer((R, HD), BF16), buffer((R, HD), BF16), buffer((R, HD), BF16), buffer((R, HD), BF16),
        buffer((R, HD), F32), buffer((R, HD), F32),
        buffer((R, HD), BF16), buffer((R, HD), BF16), buffer((R, HD), BF16), buffer((R, HD), BF16),
        buffer((R, HD), F32), buffer((R, HD), F32), buffer((R, HD), F32),
        buffer((D, half), F32), buffer((D, half), BF16), buffer((D, half), BF16),
        buffer((GROUPS, 64, half), BF16), buffer((GROUPS, 64, half), BF16),
        buffer((64, half), F32), buffer((32, half), F32), buffer((128, 128), F32), buffer((128, 128), BF16),
        buffer((R, 128), BF16), buffer((16, 128), F32), buffer((2, HD), F32), buffer((2, HD), F32),
        pltpu.SemaphoreType.DMA((24,)), pltpu.SemaphoreType.DMA((8,)),
        pltpu.SemaphoreType.DMA((8,)), pltpu.SemaphoreType.DMA((8,)),
    ]
    kinds = (((R, HD), BF16), ((R, D), BF16), ((R, HD), BF16), ((R, HD), BF16), ((2, HD), F32))
    inputs = (
        features, query_rows, key_rows, w_value, cotangent,
        station.reshape(1, R), bucket.reshape(1, R), slot_index.reshape(1, R),
    )
    results = pl.pallas_call(
        kernel,
        out_shape=tuple(pltpu.VMEM(*kind) for kind in kinds),
        in_specs=[pl.BlockSpec(memory_space=pltpu.HBM)] * 8,
        out_specs=(vmem,) * 5,
        scratch_shapes=scratch,
        compiler_params=pltpu.CompilerParams(
            collective_id=0, has_side_effects=True, vmem_limit_bytes=48 * 1024 * 1024
        ),
        name="delay_attention",
    )(*(pltpu.with_memory_space_constraint(array, pltpu.HBM) for array in inputs))
    return pl.pallas_call(
        write,
        out_shape=tuple(jax.ShapeDtypeStruct(*kind) for kind in kinds),
        in_specs=[vmem] * 5,
        out_specs=(pl.BlockSpec(memory_space=pltpu.HBM),) * 5,
        scratch_shapes=[pltpu.SemaphoreType.DMA((5,))],
        name="write_results",
    )(*(pltpu.with_memory_space_constraint(array, pltpu.VMEM) for array in results))


def solution(mesh):
    rows = P(("grp", "trn"), None)
    ids = P(("grp", "trn"))
    return jax.shard_map(
        shards,
        mesh=mesh,
        in_specs=(rows,) * 5 + (ids,) * 3,
        out_specs=(rows,) * 5,
        check_vma=False,
    )
```

```python
import functools

import jax
import jax.numpy as jnp
from jax import lax
from jax.experimental import pallas as pl
from jax.experimental.pallas import tpu as pltpu
from jax.sharding import PartitionSpec as P

MESH = pl.DeviceIdType.MESH
BF16 = jnp.bfloat16
F32 = jnp.float32
I32 = jnp.int32
HEADS = 8
HDIM = 64
HD = 512
D = 1024
R = 256
WIN = 128
MEMBERS = 32
GROUPS = 16
CHIPS = 16
NEG = -1e30


def dot(a, b):
    return lax.dot_general(a, b, (((1,), (0,)), ((), ())), preferred_element_type=F32)


def dot_nt(a, b):
    return lax.dot_general(a, b, (((1,), (1,)), ((), ())), preferred_element_type=F32)


def dot_tn(a, b):
    return lax.dot_general(a, b, (((0,), (0,)), ((), ())), preferred_element_type=F32)


def iota(shape, dim):
    return lax.broadcasted_iota(I32, shape, dim)


def to_col(row):
    eye = iota((R, R), 0) == iota((R, R), 1)
    return jnp.sum(jnp.where(eye, jnp.broadcast_to(row, (R, R)), 0), axis=1, keepdims=True)


def to_row(col):
    eye = iota((R, R), 0) == iota((R, R), 1)
    return jnp.sum(jnp.where(eye, jnp.broadcast_to(col, (R, R)), 0), axis=0, keepdims=True)


def pack(rows):
    cut = rows.reshape(MEMBERS, 8, HD)
    return jnp.concatenate([cut[:, :, : HD // 2], cut[:, :, HD // 2 :]], axis=1).reshape(2 * R, HD // 2).astype(BF16)


def unpack(block):
    cut = block.astype(F32).reshape(MEMBERS, 16, HD // 2)
    low = cut[:, :8].reshape(R, HD // 2)
    high = cut[:, 8:].reshape(R, HD // 2)
    return jnp.concatenate([low, high], axis=1).astype(BF16)


def softmax(scores):
    top = jnp.max(scores, axis=1, keepdims=True)
    raised = jnp.exp(scores - top)
    return raised * (1.0 / jnp.sum(raised, axis=1, keepdims=True))


def kernel(
    feat_in, query_in, key_in, w_in, cot_in, station_in, bucket_in, slot_in,
    mixed_o, gfeat_o, gq_o, gk_o, gw_o,
    feat, query, key, w_part, cot, station, bucket, slot,
    order, restore, bias, stop_p, win_p,
    send, recv, send_m, recv_m,
    w_pair, w_block, w_send, w_recv, w_rows, w_full,
    vals, ctx, grad_c, grad_v, stop_q, stop_k,
    qw, kw, vw, dw, out_m, out_q, out_k,
    gw_own, rs0_send, rs0_recv, rs1_send, rs1_recv, rs1_sum, rs2_swap, rs2_rows, rs2_send, rs2_recv,
    rs3_rows, rs3_send, rs3_recv,
    sems, in_sems, send_sems, recv_sems, ready,
):
    copies_in = [
        pltpu.make_async_copy(source, target, in_sems.at[number])
        for number, (source, target) in enumerate((
            (slot_in, slot), (query_in, query), (w_in, w_part), (station_in, station), (bucket_in, bucket),
            (key_in, key), (cot_in, cot), (feat_in, feat),
        ))
    ]
    copies_in[0].start()
    copies_in[1].start()
    grp = lax.axis_index("grp")
    trn = lax.axis_index("trn")
    chip = trn // 2
    core = trn % 2
    sibling = chip * 2 + (1 - core)

    def member(step):
        return lax.rem(trn + step, MEMBERS)

    def group(step):
        return lax.rem(grp + step, GROUPS)

    barrier = pltpu.get_barrier_semaphore()

    def greet(group_index, member_index):
        pl.semaphore_signal(barrier, inc=1, device_id=(group_index, member_index), device_id_type=MESH)

    pl.loop(1, CHIPS)(lambda step: greet(grp, lax.rem(chip + step, CHIPS) * 2))

    @pl.when(core == 1)
    def _():
        greet(grp, sibling)

    pl.loop(1, GROUPS)(lambda step: greet(group(step), chip * 2 + 1))

    for copy in copies_in[2:]:
        copy.start()

    def all_in(first_core, count, number):
        @pl.when(core == first_core)
        def _():
            pl.semaphore_wait(barrier, count)
            pl.semaphore_signal(ready.at[number], inc=1, device_id=(grp, sibling), device_id_type=MESH)

        @pl.when(core != first_core)
        def _():
            pl.semaphore_wait(ready.at[number], 1)

    def block(number, ref, who):
        return ref.at[number, pl.ds(pl.multiple_of(who * 16, 16), 16)]

    def exchange(number, first=1, stride=1):
        if first == 1:
            pltpu.make_async_copy(block(number, send, trn), block(number, recv, trn), recv_sems.at[number]).start()

        @pl.loop(first, MEMBERS, step=stride)
        def _(step):
            peer = member(step)
            pltpu.make_async_remote_copy(
                src_ref=block(number, send, peer), dst_ref=block(number, recv, trn),
                send_sem=send_sems.at[number], recv_sem=recv_sems.at[number],
                device_id=(grp, peer), device_id_type=MESH,
            ).start()

    def wait_for(ref, sem):
        pltpu.make_async_copy(ref, ref, sems.at[sem]).wait()

    def arrived(number):
        pltpu.make_async_copy(recv.at[number], recv.at[number], recv_sems.at[number]).wait()

    def sent(number):
        blocks = send.at[number, pl.ds(0, (MEMBERS - 1) * 16)]
        pltpu.make_async_copy(blocks, blocks, send_sems.at[number]).wait()

    copies_in[0].wait()
    slot_row = slot[...]
    goal_row = slot_row // R
    goal_col = to_col(goal_row)
    same = (goal_col == goal_row) & (iota((R, R), 0) < iota((R, R), 1))
    rank_row = jnp.sum(jnp.where(same, 1, 0), axis=0, keepdims=True)
    pos_row = goal_row * 8 + rank_row
    pos_col = to_col(pos_row)
    picks = iota((R, R), 0) == pos_row
    order[...] = jnp.where(picks, 1.0, 0.0).astype(BF16)

    half = HD // 2
    copies_in[1].wait()
    send[0] = pack(dot(order[...], query[...]))
    copies_in[2].wait()
    w_pair[core] = w_part[...].astype(F32)

    all_in(0, MEMBERS - 1, 0)

    share = pltpu.make_async_remote_copy(
        src_ref=w_pair.at[core], dst_ref=w_pair.at[core], send_sem=sems.at[0], recv_sem=sems.at[1],
        device_id=(grp, sibling), device_id_type=MESH,
    )
    share.start()
    exchange(0, 1, 2)
    share.wait()
    four_rows = w_pair[...].reshape(4, HD)
    for part in range(4):
        w_block[4 * part : 4 * part + 4, :] = four_rows[:, 128 * part : 128 * part + 128]
    w_send[...] = w_block[...].astype(BF16)
    near = chip // 8
    eight = lax.rem(chip, 8)

    def part_16(ref, who):
        return ref.at[pl.ds(pl.multiple_of(who * 16, 16), 16)]

    @pl.when(core == near)
    def _():
        pltpu.make_async_copy(w_send, part_16(w_recv, eight), sems.at[9]).start()

    def send_weights(away):
        pltpu.make_async_remote_copy(
            src_ref=w_send, dst_ref=part_16(w_recv, eight), send_sem=sems.at[8], recv_sem=sems.at[9],
            device_id=(grp, lax.rem(chip + CHIPS + away, CHIPS) * 2 + near), device_id_type=MESH,
        ).start()

    pl.loop(1, 8)(lambda step: send_weights(step * (1 - 2 * core)))

    @pl.when(core == 0)
    def _():
        send_weights(8)

    exchange(0, 2, 2)
    copies_in[5].wait()
    send[1] = pack(dot(order[...], key[...]))
    exchange(1)

    copies_in[3].wait()
    copies_in[4].wait()
    lane = iota((R, 128), 1)
    within = iota((R, 128), 0) % 8

    def sorted_col(row):
        return jnp.sum(jnp.where(picks, jnp.broadcast_to(row, (R, R)), 0), axis=1, keepdims=True)

    place_col = sorted_col(slot_row % R)
    station_col = sorted_col(station[...])
    bucket_col = sorted_col(bucket[...])
    meta = (
        jnp.where(lane == within, place_col, 0)
        + jnp.where(lane == within + 8, station_col, 0)
        + jnp.where(lane == within + 16, bucket_col, 0)
    )
    send_m[...] = jnp.sum(meta.reshape(MEMBERS, 8, 128), axis=1, keepdims=True)

    def all_blocks_m(step):
        peer = member(step)
        pltpu.make_async_remote_copy(
            src_ref=send_m.at[peer], dst_ref=recv_m.at[trn], send_sem=sems.at[4], recv_sem=sems.at[5],
            device_id=(grp, peer), device_id_type=MESH,
        ).start()

    pltpu.make_async_copy(send_m.at[trn], recv_m.at[trn], sems.at[5]).start()
    pl.loop(1, MEMBERS)(all_blocks_m)

    copies_in[6].wait()
    send[2] = pack(dot(order[...], cot[...]))
    exchange(2)
    restore[...] = jnp.where(pos_col == iota((R, R), 1), 1.0, 0.0).astype(BF16)

    wait_for(w_recv, 9)
    wide = w_recv[...].astype(F32)
    for step in range(8):
        for part in range(4):
            first_row = 16 * step + 4 * part
            w_rows[4 * step : 4 * step + 4, 128 * part : 128 * part + 128] = wide[first_row : first_row + 4]
    w_full[grp, core] = w_rows[...].astype(BF16)
    all_in(1, 2 * (GROUPS - 1), 1)

    @pl.loop(1, GROUPS)
    def _(step):
        pltpu.make_async_remote_copy(
            src_ref=w_full.at[grp, core], dst_ref=w_full.at[grp, core], send_sem=sems.at[6], recv_sem=sems.at[7],
            device_id=(group(step), trn), device_id_type=MESH,
        ).start()

    low_lane = iota((R, 128), 1) < HDIM

    def heads_of(ref, pair):
        part = ref[:, pl.ds(pl.multiple_of(pair * 128, 128), 128)]
        zero = jnp.zeros_like(part)
        return part, jnp.where(low_lane, part, zero), jnp.where(low_lane, zero, part)

    def cols(pair):
        return (slice(None), pl.ds(pl.multiple_of(pair * 128, 128), 128))

    def weights_into(target, q_ref, k_ref):
        @pl.loop(0, HEADS // 2)
        def _(pair):
            k_pair = k_ref[cols(pair)]
            _, *q_heads = heads_of(q_ref, pair)
            for head in range(2):
                scores = dot_nt(q_heads[head], k_pair) * (HDIM ** -0.5) + bias[...]
                target[2 * pair + head] = softmax(scores).astype(BF16)

    bias[...] = jnp.where(iota((R, R), 1) <= iota((R, R), 0), 0.0, NEG)
    weights_into(stop_p, query, key)

    wait_for(w_full.at[pl.ds(0, GROUPS - 1), core], 7)
    wait_for(w_full.at[pl.ds(0, GROUPS - 1), core], 6)
    swap_w = pltpu.make_async_remote_copy(
        src_ref=w_full.at[:, core], dst_ref=w_full.at[:, core], send_sem=sems.at[10], recv_sem=sems.at[11],
        device_id=(grp, sibling), device_id_type=MESH,
    )
    swap_w.start()
    swap_w.wait()

    weight = w_full[...].reshape(D, HD)
    copies_in[7].wait()
    vals[...] = dot(feat[...], weight).astype(BF16)

    def attend(p_ref, v_ref, out_ref):
        @pl.loop(0, HEADS // 2)
        def _(pair):
            v_pair = v_ref[cols(pair)]
            first = dot(p_ref[2 * pair], v_pair)
            second = dot(p_ref[2 * pair + 1], v_pair)
            out_ref[cols(pair)] = jnp.where(low_lane, first, second).astype(out_ref.dtype)

    def attend_value_back(p_ref, d_ref, out_ref):
        @pl.loop(0, HEADS // 2)
        def _(pair):
            d_pair = d_ref[cols(pair)]
            first = dot_tn(p_ref[2 * pair], d_pair)
            second = dot_tn(p_ref[2 * pair + 1], d_pair)
            out_ref[cols(pair)] = jnp.where(low_lane, first, second).astype(out_ref.dtype)

    def attend_back(p_ref, q_ref, k_ref, v_ref, d_ref, dq_ref, dk_ref):
        @pl.loop(0, HEADS // 2)
        def _(pair):
            q_pair, k_pair, v_pair = q_ref[cols(pair)], k_ref[cols(pair)], v_ref[cols(pair)]
            _, *d_heads = heads_of(d_ref, pair)
            dq, dk = [], []
            for head in range(2):
                weights = p_ref[2 * pair + head].astype(F32)
                grad = dot_nt(d_heads[head], v_pair)
                row_dot = jnp.sum(weights * grad, axis=1, keepdims=True)
                grad = (weights * (grad - row_dot)).astype(BF16)
                dq.append(dot(grad, k_pair))
                dk.append(dot_tn(grad, q_pair))
            factor = HDIM ** -0.5
            dq_ref[cols(pair)] = (jnp.where(low_lane, dq[0], dq[1]) * factor).astype(dq_ref.dtype)
            dk_ref[cols(pair)] = (jnp.where(low_lane, dk[0], dk[1]) * factor).astype(dk_ref.dtype)

    attend(stop_p, vals, ctx)
    send[3] = pack(dot(order[...], ctx[...]))
    exchange(3)

    wait_for(recv_m, 5)
    got = jnp.broadcast_to(recv_m[...], (MEMBERS, 8, 128)).reshape(R, 128)

    def field(number):
        return jnp.sum(jnp.where(lane == within + 8 * number, got, 0), axis=1, keepdims=True)

    piece = field(1) * 2 + field(0) // WIN
    buckets = field(2)
    allowed = (piece == to_row(piece)) & (to_row(buckets) <= buckets)
    bias[...] = jnp.where(allowed, 0.0, NEG)
    arrived(0)
    qw[...] = unpack(recv[0])
    arrived(1)
    kw[...] = unpack(recv[1])
    weights_into(win_p, qw, kw)
    arrived(2)
    dw[...] = unpack(recv[2])
    attend_value_back(win_p, dw, out_m)
    send[4] = pack(out_m[...])
    exchange(4)

    arrived(3)
    vw[...] = unpack(recv[3])
    attend(win_p, vw, out_m)
    send[5] = pack(out_m[...])
    exchange(5)
    attend_back(win_p, qw, kw, vw, dw, out_q, out_k)
    send[6] = pack(out_q[...])
    exchange(6)
    send[7] = pack(out_k[...])

    def put_back(number):
        arrived(number)
        return dot(restore[...], unpack(recv[number]))

    grad_c[...] = put_back(4).astype(BF16)
    attend_value_back(stop_p, grad_c, grad_v)

    mine = (slice(None), pl.ds(pl.multiple_of(core * half, half), half))
    other = (slice(None), pl.ds(pl.multiple_of((1 - core) * half, half), half))
    rs0_send[...] = dot_tn(feat[...], grad_v[other]).astype(BF16)
    swap_0 = pltpu.make_async_remote_copy(
        src_ref=rs0_send, dst_ref=rs0_recv, send_sem=sems.at[16], recv_sem=sems.at[17],
        device_id=(grp, sibling), device_id_type=MESH,
    )
    swap_0.start()
    gw_own[...] = dot_tn(feat[...], grad_v[mine])
    swap_0.wait()
    rs1_send[...] = (gw_own[...] + rs0_recv[...].astype(F32)).astype(BF16).reshape(GROUPS, 64, half)
    rs1_recv[grp] = rs1_send[grp]

    @pl.loop(1, GROUPS)
    def _(step):
        peer = group(step)
        pltpu.make_async_remote_copy(
            src_ref=rs1_send.at[peer], dst_ref=rs1_recv.at[grp], send_sem=sems.at[18], recv_sem=sems.at[19],
            device_id=(peer, trn), device_id_type=MESH,
        ).start()

    exchange(7, 1, 2)
    attend_back(stop_p, query, key, vals, grad_c, stop_q, stop_k)

    wait_for(rs1_recv.at[pl.ds(0, GROUPS - 1)], 19)
    total = rs1_recv[0].astype(F32)
    for step in range(1, GROUPS):
        total = total + rs1_recv[step].astype(F32)
    rs1_sum[...] = total

    swap_2 = pltpu.make_async_remote_copy(
        src_ref=rs1_sum.at[pl.ds(pl.multiple_of(32 * (1 - core), 32), 32)], dst_ref=rs2_swap,
        send_sem=sems.at[20], recv_sem=sems.at[21], device_id=(grp, sibling), device_id_type=MESH,
    )
    swap_2.start()
    gfeat_o[...] = dot_nt(grad_v[...], w_full[...].reshape(D, HD)).astype(BF16)
    swap_2.wait()
    is_first = core == 0
    kept = rs1_sum[pl.ds(pl.multiple_of(32 * core, 32), 32), :]
    swapped = rs2_swap[...]
    sides = (jnp.where(is_first, kept, swapped), jnp.where(is_first, swapped, kept))
    for step in range(CHIPS // 2):
        for part in range(4):
            piece_4 = sides[part // 2][4 * step : 4 * step + 4, 128 * (part % 2) : 128 * (part % 2) + 128]
            rs2_rows[16 * step + 4 * part : 16 * step + 4 * part + 4, :] = piece_4
    rs2_send[...] = rs2_rows[...].astype(BF16)

    summing = core == near

    @pl.when(summing)
    def _():
        pltpu.make_async_copy(part_16(rs2_send, eight), part_16(rs2_recv, chip), sems.at[23]).start()

    @pl.when(jnp.logical_not(summing))
    def _():
        pltpu.make_async_remote_copy(
            src_ref=part_16(rs2_send, eight), dst_ref=part_16(rs2_recv, chip),
            send_sem=sems.at[22], recv_sem=sems.at[23],
            device_id=(grp, (8 * core + eight) * 2 + core), device_id_type=MESH,
        ).start()

    @pl.loop(1, 8)
    def _(step):
        peer = lax.rem(eight + step, 8)
        pltpu.make_async_remote_copy(
            src_ref=part_16(rs2_send, peer), dst_ref=part_16(rs2_recv, chip),
            send_sem=sems.at[22], recv_sem=sems.at[23],
            device_id=(grp, (8 * core + peer) * 2 + core), device_id_type=MESH,
        ).start()

    exchange(7, 2, 2)

    mixed_o[...] = put_back(5).astype(BF16)
    gq_o[...] = (stop_q[...] + put_back(6)).astype(BF16)

    give = pltpu.make_async_remote_copy(
        src_ref=rs3_send, dst_ref=rs3_recv, send_sem=sems.at[2], recv_sem=sems.at[3],
        device_id=(grp, sibling), device_id_type=MESH,
    )

    @pl.when(summing)
    def _():
        wait_for(rs2_recv, 23)
        rows_16 = jnp.sum(rs2_recv[...].astype(F32).reshape(CHIPS, 16, 128), axis=0)
        rs3_rows[...] = rows_16 * ((R * MEMBERS * GROUPS) ** -0.5)
        four = [rs3_rows[4 * part : 4 * part + 4, :] for part in range(4)]
        rows_4 = jnp.concatenate(four, axis=1)
        rs3_send[...] = jnp.where(is_first, rows_4[2:4], rows_4[0:2])
        give.start()
        gw_o[...] = jnp.where(is_first, rows_4[0:2], rows_4[2:4])

    gk_o[...] = (stop_k[...] + put_back(7)).astype(BF16)

    @pl.when(summing)
    def _():
        give.wait_send()

    @pl.when(jnp.logical_not(summing))
    def _():
        give.wait_recv()
        gw_o[...] = rs3_recv[...]

    for number in range(8):
        sent(number)
    wait_for(send_m.at[pl.ds(0, MEMBERS - 1)], 4)
    wait_for(w_recv.at[pl.ds(0, 7 * 16)], 8)

    @pl.when(core == 0)
    def _():
        wait_for(w_send, 8)

    wait_for(rs1_send.at[pl.ds(0, GROUPS - 1)], 18)
    wait_for(rs2_send.at[pl.ds(0, 7 * 16)], 22)

    @pl.when(jnp.logical_not(summing))
    def _():
        wait_for(rs2_send.at[pl.ds(0, 16)], 22)


def write(*refs):
    *pairs, sems = refs
    copies = [
        pltpu.make_async_copy(source, target, sems.at[number])
        for number, (source, target) in enumerate(zip(pairs[:5], pairs[5:]))
    ]
    for copy in copies:
        copy.start()
    for copy in copies:
        copy.wait()


def shards(features, query_rows, key_rows, w_value, cotangent, station, bucket, slot_index):
    half = HD // 2
    vmem = pl.BlockSpec(memory_space=pltpu.VMEM)

    def buffer(shape, dtype):
        return pltpu.VMEM(shape, dtype)

    scratch = [
        buffer((R, D), BF16), buffer((R, HD), BF16), buffer((R, HD), BF16), buffer((2, HD), BF16), buffer((R, HD), BF16),
        buffer((1, R), I32), buffer((1, R), I32), buffer((1, R), I32),
        buffer((R, R), BF16), buffer((R, R), BF16), buffer((R, R), F32),
        buffer((HEADS, R, R), BF16), buffer((HEADS, R, R), BF16),
        buffer((8, 2 * R, half), BF16), buffer((8, 2 * R, half), BF16),
        buffer((MEMBERS, 1, 128), I32), buffer((MEMBERS, 1, 128), I32),
        buffer((2, 2, HD), F32), buffer((16, 128), F32), buffer((16, 128), BF16), buffer((128, 128), BF16),
        buffer((32, HD), F32), buffer((GROUPS, 2, 32, HD), BF16),
        buffer((R, HD), BF16), buffer((R, HD), BF16), buffer((R, HD), BF16), buffer((R, HD), BF16),
        buffer((R, HD), F32), buffer((R, HD), F32),
        buffer((R, HD), BF16), buffer((R, HD), BF16), buffer((R, HD), BF16), buffer((R, HD), BF16),
        buffer((R, HD), F32), buffer((R, HD), F32), buffer((R, HD), F32),
        buffer((D, half), F32), buffer((D, half), BF16), buffer((D, half), BF16),
        buffer((GROUPS, 64, half), BF16), buffer((GROUPS, 64, half), BF16),
        buffer((64, half), F32), buffer((32, half), F32), buffer((128, 128), F32), buffer((128, 128), BF16),
        buffer((R, 128), BF16), buffer((16, 128), F32), buffer((2, HD), F32), buffer((2, HD), F32),
        pltpu.SemaphoreType.DMA((24,)), pltpu.SemaphoreType.DMA((8,)),
        pltpu.SemaphoreType.DMA((8,)), pltpu.SemaphoreType.DMA((8,)), pltpu.SemaphoreType.REGULAR((2,)),
    ]
    kinds = (((R, HD), BF16), ((R, D), BF16), ((R, HD), BF16), ((R, HD), BF16), ((2, HD), F32))
    inputs = (
        features, query_rows, key_rows, w_value, cotangent,
        station.reshape(1, R), bucket.reshape(1, R), slot_index.reshape(1, R),
    )
    results = pl.pallas_call(
        kernel,
        out_shape=tuple(pltpu.VMEM(*kind) for kind in kinds),
        in_specs=[pl.BlockSpec(memory_space=pltpu.HBM)] * 8,
        out_specs=(vmem,) * 5,
        scratch_shapes=scratch,
        compiler_params=pltpu.CompilerParams(
            collective_id=0, has_side_effects=True, vmem_limit_bytes=48 * 1024 * 1024
        ),
        name="delay_attention",
    )(*(pltpu.with_memory_space_constraint(array, pltpu.HBM) for array in inputs))
    return pl.pallas_call(
        write,
        out_shape=tuple(jax.ShapeDtypeStruct(*kind) for kind in kinds),
        in_specs=[vmem] * 5,
        out_specs=(pl.BlockSpec(memory_space=pltpu.HBM),) * 5,
        scratch_shapes=[pltpu.SemaphoreType.DMA((5,))],
        name="write_results",
    )(*(pltpu.with_memory_space_constraint(array, pltpu.VMEM) for array in results))


def solution(mesh):
    rows = P(("grp", "trn"), None)
    ids = P(("grp", "trn"))
    return jax.shard_map(
        shards,
        mesh=mesh,
        in_specs=(rows,) * 5 + (ids,) * 3,
        out_specs=(rows,) * 5,
        check_vma=False,
    )
```

```python
import functools

import jax
import jax.numpy as jnp
from jax import lax
from jax.experimental import pallas as pl
from jax.experimental.pallas import tpu as pltpu
from jax.sharding import PartitionSpec as P

MESH = pl.DeviceIdType.MESH
BF16 = jnp.bfloat16
F32 = jnp.float32
I32 = jnp.int32
HEADS = 8
HDIM = 64
HD = 512
D = 1024
R = 256
WIN = 128
MEMBERS = 32
GROUPS = 16
CHIPS = 16
NEG = -1e30


def dot(a, b):
    return lax.dot_general(a, b, (((1,), (0,)), ((), ())), preferred_element_type=F32)


def dot_nt(a, b):
    return lax.dot_general(a, b, (((1,), (1,)), ((), ())), preferred_element_type=F32)


def dot_tn(a, b):
    return lax.dot_general(a, b, (((0,), (0,)), ((), ())), preferred_element_type=F32)


def iota(shape, dim):
    return lax.broadcasted_iota(I32, shape, dim)


def to_col(row):
    eye = iota((R, R), 0) == iota((R, R), 1)
    return jnp.sum(jnp.where(eye, jnp.broadcast_to(row, (R, R)), 0), axis=1, keepdims=True)


def to_row(col):
    eye = iota((R, R), 0) == iota((R, R), 1)
    return jnp.sum(jnp.where(eye, jnp.broadcast_to(col, (R, R)), 0), axis=0, keepdims=True)


def pack(rows):
    cut = rows.reshape(MEMBERS, 8, HD)
    return jnp.concatenate([cut[:, :, : HD // 2], cut[:, :, HD // 2 :]], axis=1).reshape(2 * R, HD // 2).astype(BF16)


def unpack(block):
    cut = block.astype(F32).reshape(MEMBERS, 16, HD // 2)
    low = cut[:, :8].reshape(R, HD // 2)
    high = cut[:, 8:].reshape(R, HD // 2)
    return jnp.concatenate([low, high], axis=1).astype(BF16)


def softmax(scores):
    top = jnp.max(scores, axis=1, keepdims=True)
    raised = jnp.exp(scores - top)
    return raised * (1.0 / jnp.sum(raised, axis=1, keepdims=True))


def kernel(
    feat_in, query_in, key_in, w_in, cot_in, station_in, bucket_in, slot_in,
    mixed_o, gfeat_o, gq_o, gk_o, gw_o,
    feat, query, key, w_part, cot, station, bucket, slot,
    order, restore, bias, stop_p, win_p,
    send, recv, send_m, recv_m,
    w_pair, w_block, w_send, w_recv, w_rows, w_full,
    vals, ctx, grad_c, grad_v, stop_q, stop_k,
    qw, kw, vw, dw, out_m, out_q, out_k,
    gw_own, rs0_send, rs0_recv, rs1_send, rs1_recv, rs1_sum, rs2_swap, rs2_rows, rs2_send, rs2_recv,
    rs3_rows, rs3_send, rs3_recv,
    sems, in_sems, send_sems, recv_sems, ready,
):
    copies_in = [
        pltpu.make_async_copy(source, target, in_sems.at[number])
        for number, (source, target) in enumerate((
            (slot_in, slot), (query_in, query), (w_in, w_part), (station_in, station), (bucket_in, bucket),
            (key_in, key), (cot_in, cot), (feat_in, feat),
        ))
    ]
    copies_in[0].start()
    copies_in[1].start()
    grp = lax.axis_index("grp")
    trn = lax.axis_index("trn")
    chip = trn // 2
    core = trn % 2
    sibling = chip * 2 + (1 - core)

    def member(step):
        return lax.rem(trn + step, MEMBERS)

    def group(step):
        return lax.rem(grp + step, GROUPS)

    barrier = pltpu.get_barrier_semaphore()

    def greet(group_index, member_index):
        pl.semaphore_signal(barrier, inc=1, device_id=(group_index, member_index), device_id_type=MESH)

    pl.loop(1, CHIPS)(lambda step: greet(grp, lax.rem(chip + step, CHIPS) * 2))

    @pl.when(core == 1)
    def _():
        greet(grp, sibling)

    for copy in copies_in[2:]:
        copy.start()

    def all_in(first_core, count, number):
        @pl.when(core == first_core)
        def _():
            pl.semaphore_wait(barrier, count)
            pl.semaphore_signal(ready.at[number], inc=1, device_id=(grp, sibling), device_id_type=MESH)

        @pl.when(core != first_core)
        def _():
            pl.semaphore_wait(ready.at[number], 1)

    def block(number, ref, who):
        return ref.at[number, pl.ds(pl.multiple_of(who * 16, 16), 16)]

    def exchange(number, first=1, stride=1):
        if first == 1:
            pltpu.make_async_copy(block(number, send, trn), block(number, recv, trn), recv_sems.at[number]).start()

        @pl.loop(first, MEMBERS, step=stride)
        def _(step):
            peer = member(step)
            pltpu.make_async_remote_copy(
                src_ref=block(number, send, peer), dst_ref=block(number, recv, trn),
                send_sem=send_sems.at[number], recv_sem=recv_sems.at[number],
                device_id=(grp, peer), device_id_type=MESH,
            ).start()

    def wait_for(ref, sem):
        pltpu.make_async_copy(ref, ref, sems.at[sem]).wait()

    def arrived(number):
        pltpu.make_async_copy(recv.at[number], recv.at[number], recv_sems.at[number]).wait()

    def sent(number):
        blocks = send.at[number, pl.ds(0, (MEMBERS - 1) * 16)]
        pltpu.make_async_copy(blocks, blocks, send_sems.at[number]).wait()

    copies_in[0].wait()
    slot_row = slot[...]
    goal_row = slot_row // R
    goal_col = to_col(goal_row)
    same = (goal_col == goal_row) & (iota((R, R), 0) < iota((R, R), 1))
    rank_row = jnp.sum(jnp.where(same, 1, 0), axis=0, keepdims=True)
    pos_row = goal_row * 8 + rank_row
    pos_col = to_col(pos_row)
    picks = iota((R, R), 0) == pos_row
    order[...] = jnp.where(picks, 1.0, 0.0).astype(BF16)

    half = HD // 2
    copies_in[1].wait()
    send[0] = pack(dot(order[...], query[...]))
    copies_in[2].wait()
    w_pair[core] = w_part[...].astype(F32)

    all_in(0, MEMBERS - 1, 0)

    share = pltpu.make_async_remote_copy(
        src_ref=w_pair.at[core], dst_ref=w_pair.at[core], send_sem=sems.at[0], recv_sem=sems.at[1],
        device_id=(grp, sibling), device_id_type=MESH,
    )
    share.start()
    exchange(0, 1, 2)
    share.wait()
    four_rows = w_pair[...].reshape(4, HD)
    for part in range(4):
        w_block[4 * part : 4 * part + 4, :] = four_rows[:, 128 * part : 128 * part + 128]
    w_send[...] = w_block[...].astype(BF16)
    near = chip // 8
    eight = lax.rem(chip, 8)

    def part_16(ref, who):
        return ref.at[pl.ds(pl.multiple_of(who * 16, 16), 16)]

    high, low = eight // 4, lax.rem(chip, 4)

    @pl.when(core == near)
    def _():
        pltpu.make_async_copy(w_send, w_recv.at[high, low], sems.at[9]).start()

    def send_weights(away):
        pltpu.make_async_remote_copy(
            src_ref=w_send, dst_ref=w_recv.at[high, low], send_sem=sems.at[8], recv_sem=sems.at[9],
            device_id=(grp, lax.rem(chip + CHIPS + away, CHIPS) * 2 + near), device_id_type=MESH,
        ).start()

    send_weights(4 - 8 * core)

    @pl.when(core == 0)
    def _():
        send_weights(8)

    exchange(0, 2, 2)

    wait_for(w_recv.at[:, low], 9)

    def spread_weights(away):
        pltpu.make_async_remote_copy(
            src_ref=w_recv.at[:, low], dst_ref=w_recv.at[:, low], send_sem=sems.at[24], recv_sem=sems.at[25],
            device_id=(grp, lax.rem(chip + CHIPS + away, CHIPS) * 2 + core), device_id_type=MESH,
        ).start()

    for away in (1, -1, 2 - 4 * core):
        spread_weights(away)

    pl.loop(1, GROUPS)(lambda step: greet(group(step), chip * 2 + 1))
    copies_in[5].wait()
    send[1] = pack(dot(order[...], key[...]))
    exchange(1)

    copies_in[3].wait()
    copies_in[4].wait()
    lane = iota((R, 128), 1)
    within = iota((R, 128), 0) % 8

    def sorted_col(row):
        return jnp.sum(jnp.where(picks, jnp.broadcast_to(row, (R, R)), 0), axis=1, keepdims=True)

    place_col = sorted_col(slot_row % R)
    station_col = sorted_col(station[...])
    bucket_col = sorted_col(bucket[...])
    meta = (
        jnp.where(lane == within, place_col, 0)
        + jnp.where(lane == within + 8, station_col, 0)
        + jnp.where(lane == within + 16, bucket_col, 0)
    )
    send_m[...] = jnp.sum(meta.reshape(MEMBERS, 8, 128), axis=1, keepdims=True)

    def all_blocks_m(step):
        peer = member(step)
        pltpu.make_async_remote_copy(
            src_ref=send_m.at[peer], dst_ref=recv_m.at[trn], send_sem=sems.at[4], recv_sem=sems.at[5],
            device_id=(grp, peer), device_id_type=MESH,
        ).start()

    pltpu.make_async_copy(send_m.at[trn], recv_m.at[trn], sems.at[5]).start()
    pl.loop(1, MEMBERS)(all_blocks_m)

    copies_in[6].wait()
    send[2] = pack(dot(order[...], cot[...]))
    exchange(2)
    restore[...] = jnp.where(pos_col == iota((R, R), 1), 1.0, 0.0).astype(BF16)

    wait_for(w_recv.at[:, pl.ds(0, 3)], 25)
    wide = w_recv[...].astype(F32).reshape(128, 128)
    for step in range(8):
        for part in range(4):
            first_row = 16 * step + 4 * part
            w_rows[4 * step : 4 * step + 4, 128 * part : 128 * part + 128] = wide[first_row : first_row + 4]
    w_full[grp, core] = w_rows[...].astype(BF16)
    all_in(1, 2 * (GROUPS - 1), 1)

    @pl.loop(1, GROUPS)
    def _(step):
        pltpu.make_async_remote_copy(
            src_ref=w_full.at[grp, core], dst_ref=w_full.at[grp, core], send_sem=sems.at[6], recv_sem=sems.at[7],
            device_id=(group(step), trn), device_id_type=MESH,
        ).start()

    low_lane = iota((R, 128), 1) < HDIM

    def heads_of(ref, pair):
        part = ref[:, pl.ds(pl.multiple_of(pair * 128, 128), 128)]
        zero = jnp.zeros_like(part)
        return part, jnp.where(low_lane, part, zero), jnp.where(low_lane, zero, part)

    def cols(pair):
        return (slice(None), pl.ds(pl.multiple_of(pair * 128, 128), 128))

    def weights_into(target, q_ref, k_ref):
        @pl.loop(0, HEADS // 2)
        def _(pair):
            k_pair = k_ref[cols(pair)]
            _, *q_heads = heads_of(q_ref, pair)
            for head in range(2):
                scores = dot_nt(q_heads[head], k_pair) * (HDIM ** -0.5) + bias[...]
                target[2 * pair + head] = softmax(scores).astype(BF16)

    bias[...] = jnp.where(iota((R, R), 1) <= iota((R, R), 0), 0.0, NEG)
    weights_into(stop_p, query, key)

    wait_for(w_full.at[pl.ds(0, GROUPS - 1), core], 7)
    wait_for(w_full.at[pl.ds(0, GROUPS - 1), core], 6)
    swap_w = pltpu.make_async_remote_copy(
        src_ref=w_full.at[:, core], dst_ref=w_full.at[:, core], send_sem=sems.at[10], recv_sem=sems.at[11],
        device_id=(grp, sibling), device_id_type=MESH,
    )
    swap_w.start()
    swap_w.wait()

    weight = w_full[...].reshape(D, HD)
    copies_in[7].wait()
    vals[...] = dot(feat[...], weight).astype(BF16)

    def attend(p_ref, v_ref, out_ref):
        @pl.loop(0, HEADS // 2)
        def _(pair):
            v_pair = v_ref[cols(pair)]
            first = dot(p_ref[2 * pair], v_pair)
            second = dot(p_ref[2 * pair + 1], v_pair)
            out_ref[cols(pair)] = jnp.where(low_lane, first, second).astype(out_ref.dtype)

    def attend_value_back(p_ref, d_ref, out_ref):
        @pl.loop(0, HEADS // 2)
        def _(pair):
            d_pair = d_ref[cols(pair)]
            first = dot_tn(p_ref[2 * pair], d_pair)
            second = dot_tn(p_ref[2 * pair + 1], d_pair)
            out_ref[cols(pair)] = jnp.where(low_lane, first, second).astype(out_ref.dtype)

    def attend_back(p_ref, q_ref, k_ref, v_ref, d_ref, dq_ref, dk_ref):
        @pl.loop(0, HEADS // 2)
        def _(pair):
            q_pair, k_pair, v_pair = q_ref[cols(pair)], k_ref[cols(pair)], v_ref[cols(pair)]
            _, *d_heads = heads_of(d_ref, pair)
            dq, dk = [], []
            for head in range(2):
                weights = p_ref[2 * pair + head].astype(F32)
                grad = dot_nt(d_heads[head], v_pair)
                row_dot = jnp.sum(weights * grad, axis=1, keepdims=True)
                grad = (weights * (grad - row_dot)).astype(BF16)
                dq.append(dot(grad, k_pair))
                dk.append(dot_tn(grad, q_pair))
            factor = HDIM ** -0.5
            dq_ref[cols(pair)] = (jnp.where(low_lane, dq[0], dq[1]) * factor).astype(dq_ref.dtype)
            dk_ref[cols(pair)] = (jnp.where(low_lane, dk[0], dk[1]) * factor).astype(dk_ref.dtype)

    attend(stop_p, vals, ctx)
    send[3] = pack(dot(order[...], ctx[...]))
    exchange(3)

    wait_for(recv_m, 5)
    got = jnp.broadcast_to(recv_m[...], (MEMBERS, 8, 128)).reshape(R, 128)

    def field(number):
        return jnp.sum(jnp.where(lane == within + 8 * number, got, 0), axis=1, keepdims=True)

    piece = field(1) * 2 + field(0) // WIN
    buckets = field(2)
    allowed = (piece == to_row(piece)) & (to_row(buckets) <= buckets)
    bias[...] = jnp.where(allowed, 0.0, NEG)
    arrived(0)
    qw[...] = unpack(recv[0])
    arrived(1)
    kw[...] = unpack(recv[1])
    weights_into(win_p, qw, kw)
    arrived(2)
    dw[...] = unpack(recv[2])
    attend_value_back(win_p, dw, out_m)
    send[4] = pack(out_m[...])
    exchange(4)

    arrived(3)
    vw[...] = unpack(recv[3])
    attend(win_p, vw, out_m)
    send[5] = pack(out_m[...])
    exchange(5)
    attend_back(win_p, qw, kw, vw, dw, out_q, out_k)
    send[6] = pack(out_q[...])
    exchange(6)
    send[7] = pack(out_k[...])

    def put_back(number):
        arrived(number)
        return dot(restore[...], unpack(recv[number]))

    grad_c[...] = put_back(4).astype(BF16)
    attend_value_back(stop_p, grad_c, grad_v)

    mine = (slice(None), pl.ds(pl.multiple_of(core * half, half), half))
    other = (slice(None), pl.ds(pl.multiple_of((1 - core) * half, half), half))
    rs0_send[...] = dot_tn(feat[...], grad_v[other]).astype(BF16)
    swap_0 = pltpu.make_async_remote_copy(
        src_ref=rs0_send, dst_ref=rs0_recv, send_sem=sems.at[16], recv_sem=sems.at[17],
        device_id=(grp, sibling), device_id_type=MESH,
    )
    swap_0.start()
    gw_own[...] = dot_tn(feat[...], grad_v[mine])
    swap_0.wait()
    rs1_send[...] = (gw_own[...] + rs0_recv[...].astype(F32)).astype(BF16).reshape(GROUPS, 64, half)
    rs1_recv[grp] = rs1_send[grp]

    @pl.loop(1, GROUPS)
    def _(step):
        peer = group(step)
        pltpu.make_async_remote_copy(
            src_ref=rs1_send.at[peer], dst_ref=rs1_recv.at[grp], send_sem=sems.at[18], recv_sem=sems.at[19],
            device_id=(peer, trn), device_id_type=MESH,
        ).start()

    exchange(7, 1, 2)
    attend_back(stop_p, query, key, vals, grad_c, stop_q, stop_k)

    wait_for(rs1_recv.at[pl.ds(0, GROUPS - 1)], 19)
    total = rs1_recv[0].astype(F32)
    for step in range(1, GROUPS):
        total = total + rs1_recv[step].astype(F32)
    rs1_sum[...] = total

    swap_2 = pltpu.make_async_remote_copy(
        src_ref=rs1_sum.at[pl.ds(pl.multiple_of(32 * (1 - core), 32), 32)], dst_ref=rs2_swap,
        send_sem=sems.at[20], recv_sem=sems.at[21], device_id=(grp, sibling), device_id_type=MESH,
    )
    swap_2.start()
    gfeat_o[...] = dot_nt(grad_v[...], w_full[...].reshape(D, HD)).astype(BF16)
    swap_2.wait()
    is_first = core == 0
    kept = rs1_sum[pl.ds(pl.multiple_of(32 * core, 32), 32), :]
    swapped = rs2_swap[...]
    sides = (jnp.where(is_first, kept, swapped), jnp.where(is_first, swapped, kept))
    for step in range(CHIPS // 2):
        for part in range(4):
            piece_4 = sides[part // 2][4 * step : 4 * step + 4, 128 * (part % 2) : 128 * (part % 2) + 128]
            rs2_rows[16 * step + 4 * part : 16 * step + 4 * part + 4, :] = piece_4
    rs2_send[...] = rs2_rows[...].astype(BF16)

    summing = core == near

    @pl.when(summing)
    def _():
        pltpu.make_async_copy(part_16(rs2_send, eight), part_16(rs2_recv, chip), sems.at[23]).start()

    @pl.when(jnp.logical_not(summing))
    def _():
        pltpu.make_async_remote_copy(
            src_ref=part_16(rs2_send, eight), dst_ref=part_16(rs2_recv, chip),
            send_sem=sems.at[22], recv_sem=sems.at[23],
            device_id=(grp, (8 * core + eight) * 2 + core), device_id_type=MESH,
        ).start()

    @pl.loop(1, 8)
    def _(step):
        peer = lax.rem(eight + step, 8)
        pltpu.make_async_remote_copy(
            src_ref=part_16(rs2_send, peer), dst_ref=part_16(rs2_recv, chip),
            send_sem=sems.at[22], recv_sem=sems.at[23],
            device_id=(grp, (8 * core + peer) * 2 + core), device_id_type=MESH,
        ).start()

    exchange(7, 2, 2)

    mixed_o[...] = put_back(5).astype(BF16)
    gq_o[...] = (stop_q[...] + put_back(6)).astype(BF16)

    give = pltpu.make_async_remote_copy(
        src_ref=rs3_send, dst_ref=rs3_recv, send_sem=sems.at[2], recv_sem=sems.at[3],
        device_id=(grp, sibling), device_id_type=MESH,
    )

    @pl.when(summing)
    def _():
        wait_for(rs2_recv, 23)
        rows_16 = jnp.sum(rs2_recv[...].astype(F32).reshape(CHIPS, 16, 128), axis=0)
        rs3_rows[...] = rows_16 * ((R * MEMBERS * GROUPS) ** -0.5)
        four = [rs3_rows[4 * part : 4 * part + 4, :] for part in range(4)]
        rows_4 = jnp.concatenate(four, axis=1)
        rs3_send[...] = jnp.where(is_first, rows_4[2:4], rows_4[0:2])
        give.start()
        gw_o[...] = jnp.where(is_first, rows_4[0:2], rows_4[2:4])

    gk_o[...] = (stop_k[...] + put_back(7)).astype(BF16)

    @pl.when(summing)
    def _():
        give.wait_send()

    @pl.when(jnp.logical_not(summing))
    def _():
        give.wait_recv()
        gw_o[...] = rs3_recv[...]

    for number in range(8):
        sent(number)
    wait_for(send_m.at[pl.ds(0, MEMBERS - 1)], 4)
    wait_for(w_send, 8)

    @pl.when(core == 0)
    def _():
        wait_for(w_send, 8)

    wait_for(w_recv.at[:, pl.ds(0, 3)], 24)
    wait_for(rs1_send.at[pl.ds(0, GROUPS - 1)], 18)
    wait_for(rs2_send.at[pl.ds(0, 7 * 16)], 22)

    @pl.when(jnp.logical_not(summing))
    def _():
        wait_for(rs2_send.at[pl.ds(0, 16)], 22)


def write(*refs):
    *pairs, sems = refs
    copies = [
        pltpu.make_async_copy(source, target, sems.at[number])
        for number, (source, target) in enumerate(zip(pairs[:5], pairs[5:]))
    ]
    for copy in copies:
        copy.start()
    for copy in copies:
        copy.wait()


def shards(features, query_rows, key_rows, w_value, cotangent, station, bucket, slot_index):
    half = HD // 2
    vmem = pl.BlockSpec(memory_space=pltpu.VMEM)

    def buffer(shape, dtype):
        return pltpu.VMEM(shape, dtype)

    scratch = [
        buffer((R, D), BF16), buffer((R, HD), BF16), buffer((R, HD), BF16), buffer((2, HD), BF16), buffer((R, HD), BF16),
        buffer((1, R), I32), buffer((1, R), I32), buffer((1, R), I32),
        buffer((R, R), BF16), buffer((R, R), BF16), buffer((R, R), F32),
        buffer((HEADS, R, R), BF16), buffer((HEADS, R, R), BF16),
        buffer((8, 2 * R, half), BF16), buffer((8, 2 * R, half), BF16),
        buffer((MEMBERS, 1, 128), I32), buffer((MEMBERS, 1, 128), I32),
        buffer((2, 2, HD), F32), buffer((16, 128), F32), buffer((16, 128), BF16), buffer((2, 4, 16, 128), BF16),
        buffer((32, HD), F32), buffer((GROUPS, 2, 32, HD), BF16),
        buffer((R, HD), BF16), buffer((R, HD), BF16), buffer((R, HD), BF16), buffer((R, HD), BF16),
        buffer((R, HD), F32), buffer((R, HD), F32),
        buffer((R, HD), BF16), buffer((R, HD), BF16), buffer((R, HD), BF16), buffer((R, HD), BF16),
        buffer((R, HD), F32), buffer((R, HD), F32), buffer((R, HD), F32),
        buffer((D, half), F32), buffer((D, half), BF16), buffer((D, half), BF16),
        buffer((GROUPS, 64, half), BF16), buffer((GROUPS, 64, half), BF16),
        buffer((64, half), F32), buffer((32, half), F32), buffer((128, 128), F32), buffer((128, 128), BF16),
        buffer((R, 128), BF16), buffer((16, 128), F32), buffer((2, HD), F32), buffer((2, HD), F32),
        pltpu.SemaphoreType.DMA((26,)), pltpu.SemaphoreType.DMA((8,)),
        pltpu.SemaphoreType.DMA((8,)), pltpu.SemaphoreType.DMA((8,)), pltpu.SemaphoreType.REGULAR((2,)),
    ]
    kinds = (((R, HD), BF16), ((R, D), BF16), ((R, HD), BF16), ((R, HD), BF16), ((2, HD), F32))
    inputs = (
        features, query_rows, key_rows, w_value, cotangent,
        station.reshape(1, R), bucket.reshape(1, R), slot_index.reshape(1, R),
    )
    results = pl.pallas_call(
        kernel,
        out_shape=tuple(pltpu.VMEM(*kind) for kind in kinds),
        in_specs=[pl.BlockSpec(memory_space=pltpu.HBM)] * 8,
        out_specs=(vmem,) * 5,
        scratch_shapes=scratch,
        compiler_params=pltpu.CompilerParams(
            collective_id=0, has_side_effects=True, vmem_limit_bytes=48 * 1024 * 1024
        ),
        name="delay_attention",
    )(*(pltpu.with_memory_space_constraint(array, pltpu.HBM) for array in inputs))
    return pl.pallas_call(
        write,
        out_shape=tuple(jax.ShapeDtypeStruct(*kind) for kind in kinds),
        in_specs=[vmem] * 5,
        out_specs=(pl.BlockSpec(memory_space=pltpu.HBM),) * 5,
        scratch_shapes=[pltpu.SemaphoreType.DMA((5,))],
        name="write_results",
    )(*(pltpu.with_memory_space_constraint(array, pltpu.VMEM) for array in results))


def solution(mesh):
    rows = P(("grp", "trn"), None)
    ids = P(("grp", "trn"))
    return jax.shard_map(
        shards,
        mesh=mesh,
        in_specs=(rows,) * 5 + (ids,) * 3,
        out_specs=(rows,) * 5,
        check_vma=False,
    )
```

```python
import functools

import jax
import jax.numpy as jnp
from jax import lax
from jax.experimental import pallas as pl
from jax.experimental.pallas import tpu as pltpu
from jax.sharding import PartitionSpec as P

MESH = pl.DeviceIdType.MESH
BF16 = jnp.bfloat16
F32 = jnp.float32
I32 = jnp.int32
HEADS = 8
HDIM = 64
HD = 512
D = 1024
R = 256
WIN = 128
MEMBERS = 32
GROUPS = 16
CHIPS = 16
NEG = -1e30


def dot(a, b):
    return lax.dot_general(a, b, (((1,), (0,)), ((), ())), preferred_element_type=F32)


def dot_nt(a, b):
    return lax.dot_general(a, b, (((1,), (1,)), ((), ())), preferred_element_type=F32)


def dot_tn(a, b):
    return lax.dot_general(a, b, (((0,), (0,)), ((), ())), preferred_element_type=F32)


def iota(shape, dim):
    return lax.broadcasted_iota(I32, shape, dim)


def to_col(row):
    eye = iota((R, R), 0) == iota((R, R), 1)
    return jnp.sum(jnp.where(eye, jnp.broadcast_to(row, (R, R)), 0), axis=1, keepdims=True)


def to_row(col):
    eye = iota((R, R), 0) == iota((R, R), 1)
    return jnp.sum(jnp.where(eye, jnp.broadcast_to(col, (R, R)), 0), axis=0, keepdims=True)


def pack(rows):
    cut = rows.reshape(MEMBERS, 8, HD)
    return jnp.concatenate([cut[:, :, : HD // 2], cut[:, :, HD // 2 :]], axis=1).reshape(2 * R, HD // 2).astype(BF16)


def unpack(block):
    cut = block.astype(F32).reshape(MEMBERS, 16, HD // 2)
    low = cut[:, :8].reshape(R, HD // 2)
    high = cut[:, 8:].reshape(R, HD // 2)
    return jnp.concatenate([low, high], axis=1).astype(BF16)


def softmax(scores):
    top = jnp.max(scores, axis=1, keepdims=True)
    raised = jnp.exp(scores - top)
    return raised * (1.0 / jnp.sum(raised, axis=1, keepdims=True))


def kernel(
    feat_in, query_in, key_in, w_in, cot_in, station_in, bucket_in, slot_in,
    mixed_o, gfeat_o, gq_o, gk_o, gw_o,
    feat, query, key, w_part, cot, station, bucket, slot,
    order, restore, bias, stop_p, win_p,
    send, recv, send_m, recv_m,
    w_pair, w_block, w_send, w_recv, w_rows, w_full,
    vals, ctx, grad_c, grad_v, stop_q, stop_k,
    qw, kw, vw, dw, out_m, out_q, out_k,
    gw_own, rs0_send, rs0_recv, rs1_send, rs1_recv, rs1_sum, rs2_swap, rs2_rows, rs2_send, rs2_recv,
    rs3_rows, rs3_send, rs3_recv,
    sems, in_sems, send_sems, recv_sems, ready,
):
    copies_in = [
        pltpu.make_async_copy(source, target, in_sems.at[number])
        for number, (source, target) in enumerate((
            (slot_in, slot), (query_in, query), (w_in, w_part), (station_in, station), (bucket_in, bucket),
            (key_in, key), (cot_in, cot), (feat_in, feat),
        ))
    ]
    copies_in[0].start()
    copies_in[1].start()
    grp = lax.axis_index("grp")
    trn = lax.axis_index("trn")
    chip = trn // 2
    core = trn % 2
    sibling = chip * 2 + (1 - core)

    def member(step):
        return lax.rem(trn + step, MEMBERS)

    def group(step):
        return lax.rem(grp + step, GROUPS)

    barrier = pltpu.get_barrier_semaphore()

    def greet(group_index, member_index):
        pl.semaphore_signal(barrier, inc=1, device_id=(group_index, member_index), device_id_type=MESH)

    pl.loop(1, CHIPS)(lambda step: greet(grp, lax.rem(chip + step, CHIPS) * 2))

    @pl.when(core == 1)
    def _():
        greet(grp, sibling)

    for copy in copies_in[2:]:
        copy.start()

    def all_in(first_core, count, number):
        @pl.when(core == first_core)
        def _():
            pl.semaphore_wait(barrier, count)
            pl.semaphore_signal(ready.at[number], inc=1, device_id=(grp, sibling), device_id_type=MESH)

        @pl.when(core != first_core)
        def _():
            pl.semaphore_wait(ready.at[number], 1)

    def block(number, ref, who):
        return ref.at[number, pl.ds(pl.multiple_of(who * 16, 16), 16)]

    def exchange(number, first=1, stride=1):
        if first == 1:
            pltpu.make_async_copy(block(number, send, trn), block(number, recv, trn), recv_sems.at[number]).start()

        @pl.loop(first, MEMBERS, step=stride)
        def _(step):
            peer = member(step)
            pltpu.make_async_remote_copy(
                src_ref=block(number, send, peer), dst_ref=block(number, recv, trn),
                send_sem=send_sems.at[number], recv_sem=recv_sems.at[number],
                device_id=(grp, peer), device_id_type=MESH,
            ).start()

    def wait_for(ref, sem):
        pltpu.make_async_copy(ref, ref, sems.at[sem]).wait()

    def arrived(number):
        pltpu.make_async_copy(recv.at[number], recv.at[number], recv_sems.at[number]).wait()

    def sent(number):
        blocks = send.at[number, pl.ds(0, (MEMBERS - 1) * 16)]
        pltpu.make_async_copy(blocks, blocks, send_sems.at[number]).wait()

    copies_in[0].wait()
    slot_row = slot[...]
    goal_row = slot_row // R
    goal_col = to_col(goal_row)
    same = (goal_col == goal_row) & (iota((R, R), 0) < iota((R, R), 1))
    rank_row = jnp.sum(jnp.where(same, 1, 0), axis=0, keepdims=True)
    pos_row = goal_row * 8 + rank_row
    pos_col = to_col(pos_row)
    picks = iota((R, R), 0) == pos_row
    order[...] = jnp.where(picks, 1.0, 0.0).astype(BF16)

    half = HD // 2
    copies_in[1].wait()
    send[0] = pack(dot(order[...], query[...]))
    copies_in[2].wait()
    w_pair[core] = w_part[...].astype(F32)

    all_in(0, MEMBERS - 1, 0)

    share = pltpu.make_async_remote_copy(
        src_ref=w_pair.at[core], dst_ref=w_pair.at[core], send_sem=sems.at[0], recv_sem=sems.at[1],
        device_id=(grp, sibling), device_id_type=MESH,
    )
    share.start()
    exchange(0, 1, 2)
    share.wait()
    four_rows = w_pair[...].reshape(4, HD)
    for part in range(4):
        w_block[4 * part : 4 * part + 4, :] = four_rows[:, 128 * part : 128 * part + 128]
    w_send[...] = w_block[...].astype(BF16)
    near = chip // 8
    eight = lax.rem(chip, 8)

    def part_16(ref, who):
        return ref.at[pl.ds(pl.multiple_of(who * 16, 16), 16)]

    high, low = eight // 4, lax.rem(chip, 4)

    @pl.when(core == near)
    def _():
        pltpu.make_async_copy(w_send, w_recv.at[high, low], sems.at[9]).start()

    def send_weights(away):
        pltpu.make_async_remote_copy(
            src_ref=w_send, dst_ref=w_recv.at[high, low], send_sem=sems.at[8], recv_sem=sems.at[9],
            device_id=(grp, lax.rem(chip + CHIPS + away, CHIPS) * 2 + near), device_id_type=MESH,
        ).start()

    send_weights(4 - 8 * core)

    @pl.when(core == 0)
    def _():
        send_weights(8)

    exchange(0, 2, 2)

    wait_for(w_recv.at[:, low], 9)

    def spread_weights(away):
        pltpu.make_async_remote_copy(
            src_ref=w_recv.at[:, low], dst_ref=w_recv.at[:, low], send_sem=sems.at[24], recv_sem=sems.at[25],
            device_id=(grp, lax.rem(chip + CHIPS + away, CHIPS) * 2 + core), device_id_type=MESH,
        ).start()

    for away in (1, -1, 2 - 4 * core):
        spread_weights(away)

    pl.loop(1, GROUPS)(lambda step: greet(group(step), chip * 2 + 1))
    copies_in[5].wait()
    send[1] = pack(dot(order[...], key[...]))
    exchange(1)

    copies_in[3].wait()
    copies_in[4].wait()
    lane = iota((R, 128), 1)
    within = iota((R, 128), 0) % 8

    def sorted_col(row):
        return jnp.sum(jnp.where(picks, jnp.broadcast_to(row, (R, R)), 0), axis=1, keepdims=True)

    place_col = sorted_col(slot_row % R)
    station_col = sorted_col(station[...])
    bucket_col = sorted_col(bucket[...])
    meta = (
        jnp.where(lane == within, place_col, 0)
        + jnp.where(lane == within + 8, station_col, 0)
        + jnp.where(lane == within + 16, bucket_col, 0)
    )
    send_m[...] = jnp.sum(meta.reshape(MEMBERS, 8, 128), axis=1, keepdims=True)

    def all_blocks_m(step):
        peer = member(step)
        pltpu.make_async_remote_copy(
            src_ref=send_m.at[peer], dst_ref=recv_m.at[trn], send_sem=sems.at[4], recv_sem=sems.at[5],
            device_id=(grp, peer), device_id_type=MESH,
        ).start()

    pltpu.make_async_copy(send_m.at[trn], recv_m.at[trn], sems.at[5]).start()
    pl.loop(1, MEMBERS)(all_blocks_m)

    copies_in[6].wait()
    send[2] = pack(dot(order[...], cot[...]))
    exchange(2)
    restore[...] = jnp.where(pos_col == iota((R, R), 1), 1.0, 0.0).astype(BF16)

    wait_for(w_recv.at[:, pl.ds(0, 3)], 25)
    wide = w_recv[...].astype(F32).reshape(128, 128)
    for step in range(8):
        for part in range(4):
            first_row = 16 * step + 4 * part
            w_rows[4 * step : 4 * step + 4, 128 * part : 128 * part + 128] = wide[first_row : first_row + 4]
    w_full[grp, core] = w_rows[...].astype(BF16)
    all_in(1, 2 * (GROUPS - 1), 1)

    @pl.loop(1, GROUPS)
    def _(step):
        pltpu.make_async_remote_copy(
            src_ref=w_full.at[grp, core], dst_ref=w_full.at[grp, core], send_sem=sems.at[6], recv_sem=sems.at[7],
            device_id=(group(step), trn), device_id_type=MESH,
        ).start()

    low_lane = iota((R, 128), 1) < HDIM

    def heads_of(ref, pair):
        part = ref[:, pl.ds(pl.multiple_of(pair * 128, 128), 128)]
        zero = jnp.zeros_like(part)
        return part, jnp.where(low_lane, part, zero), jnp.where(low_lane, zero, part)

    def cols(pair):
        return (slice(None), pl.ds(pl.multiple_of(pair * 128, 128), 128))

    def weights_into(target, q_ref, k_ref):
        @pl.loop(0, HEADS // 2)
        def _(pair):
            k_pair = k_ref[cols(pair)]
            _, *q_heads = heads_of(q_ref, pair)
            for head in range(2):
                scores = dot_nt(q_heads[head], k_pair) * (HDIM ** -0.5) + bias[...]
                target[2 * pair + head] = softmax(scores).astype(BF16)

    bias[...] = jnp.where(iota((R, R), 1) <= iota((R, R), 0), 0.0, NEG)
    weights_into(stop_p, query, key)

    wait_for(w_full.at[pl.ds(0, GROUPS - 1), core], 7)
    wait_for(w_full.at[pl.ds(0, GROUPS - 1), core], 6)
    swap_w = pltpu.make_async_remote_copy(
        src_ref=w_full.at[:, core], dst_ref=w_full.at[:, core], send_sem=sems.at[10], recv_sem=sems.at[11],
        device_id=(grp, sibling), device_id_type=MESH,
    )
    swap_w.start()
    swap_w.wait()

    weight = w_full[...].reshape(D, HD)
    copies_in[7].wait()
    vals[...] = dot(feat[...], weight).astype(BF16)

    def attend(p_ref, v_ref, out_ref):
        @pl.loop(0, HEADS // 2)
        def _(pair):
            v_pair = v_ref[cols(pair)]
            first = dot(p_ref[2 * pair], v_pair)
            second = dot(p_ref[2 * pair + 1], v_pair)
            out_ref[cols(pair)] = jnp.where(low_lane, first, second).astype(out_ref.dtype)

    def attend_value_back(p_ref, d_ref, out_ref):
        @pl.loop(0, HEADS // 2)
        def _(pair):
            d_pair = d_ref[cols(pair)]
            first = dot_tn(p_ref[2 * pair], d_pair)
            second = dot_tn(p_ref[2 * pair + 1], d_pair)
            out_ref[cols(pair)] = jnp.where(low_lane, first, second).astype(out_ref.dtype)

    def attend_back(p_ref, q_ref, k_ref, v_ref, d_ref, dq_ref, dk_ref):
        @pl.loop(0, HEADS // 2)
        def _(pair):
            q_pair, k_pair, v_pair = q_ref[cols(pair)], k_ref[cols(pair)], v_ref[cols(pair)]
            _, *d_heads = heads_of(d_ref, pair)
            dq, dk = [], []
            for head in range(2):
                weights = p_ref[2 * pair + head].astype(F32)
                grad = dot_nt(d_heads[head], v_pair)
                row_dot = jnp.sum(weights * grad, axis=1, keepdims=True)
                grad = (weights * (grad - row_dot)).astype(BF16)
                dq.append(dot(grad, k_pair))
                dk.append(dot_tn(grad, q_pair))
            factor = HDIM ** -0.5
            dq_ref[cols(pair)] = (jnp.where(low_lane, dq[0], dq[1]) * factor).astype(dq_ref.dtype)
            dk_ref[cols(pair)] = (jnp.where(low_lane, dk[0], dk[1]) * factor).astype(dk_ref.dtype)

    attend(stop_p, vals, ctx)
    send[3] = pack(dot(order[...], ctx[...]))
    exchange(3)

    wait_for(recv_m, 5)
    got = jnp.broadcast_to(recv_m[...], (MEMBERS, 8, 128)).reshape(R, 128)

    def field(number):
        return jnp.sum(jnp.where(lane == within + 8 * number, got, 0), axis=1, keepdims=True)

    piece = field(1) * 2 + field(0) // WIN
    buckets = field(2)
    allowed = (piece == to_row(piece)) & (to_row(buckets) <= buckets)
    bias[...] = jnp.where(allowed, 0.0, NEG)
    arrived(0)
    qw[...] = unpack(recv[0])
    arrived(1)
    kw[...] = unpack(recv[1])
    weights_into(win_p, qw, kw)
    arrived(2)
    dw[...] = unpack(recv[2])
    attend_value_back(win_p, dw, out_m)
    send[4] = pack(out_m[...])
    exchange(4)

    arrived(3)
    vw[...] = unpack(recv[3])
    attend(win_p, vw, out_m)
    send[5] = pack(out_m[...])
    exchange(5)
    attend_back(win_p, qw, kw, vw, dw, out_q, out_k)
    send[6] = pack(out_q[...])
    exchange(6)
    send[7] = pack(out_k[...])

    def put_back(number):
        arrived(number)
        return dot(restore[...], unpack(recv[number]))

    grad_c[...] = put_back(4).astype(BF16)
    attend_value_back(stop_p, grad_c, grad_v)

    mine = (slice(None), pl.ds(pl.multiple_of(core * half, half), half))
    other = (slice(None), pl.ds(pl.multiple_of((1 - core) * half, half), half))
    rs0_send[...] = dot_tn(feat[...], grad_v[other]).astype(BF16)
    swap_0 = pltpu.make_async_remote_copy(
        src_ref=rs0_send, dst_ref=rs0_recv, send_sem=sems.at[16], recv_sem=sems.at[17],
        device_id=(grp, sibling), device_id_type=MESH,
    )
    swap_0.start()
    gw_own[...] = dot_tn(feat[...], grad_v[mine])
    swap_0.wait()
    rs1_send[...] = (gw_own[...] + rs0_recv[...].astype(F32)).astype(BF16).reshape(GROUPS, 64, half)
    rs1_recv[grp] = rs1_send[grp]

    @pl.loop(1, GROUPS)
    def _(step):
        peer = group(step)
        pltpu.make_async_remote_copy(
            src_ref=rs1_send.at[peer], dst_ref=rs1_recv.at[grp], send_sem=sems.at[18], recv_sem=sems.at[19],
            device_id=(peer, trn), device_id_type=MESH,
        ).start()

    exchange(7, 1, 2)
    attend_back(stop_p, query, key, vals, grad_c, stop_q, stop_k)

    wait_for(rs1_recv.at[pl.ds(0, GROUPS - 1)], 19)
    total = rs1_recv[0].astype(F32)
    for step in range(1, GROUPS):
        total = total + rs1_recv[step].astype(F32)
    rs1_sum[...] = total

    swap_2 = pltpu.make_async_remote_copy(
        src_ref=rs1_sum.at[pl.ds(pl.multiple_of(32 * (1 - core), 32), 32)], dst_ref=rs2_swap,
        send_sem=sems.at[20], recv_sem=sems.at[21], device_id=(grp, sibling), device_id_type=MESH,
    )
    swap_2.start()
    exchange(7, 2, 4)
    gfeat_o[...] = dot_nt(grad_v[...], w_full[...].reshape(D, HD)).astype(BF16)
    swap_2.wait()
    is_first = core == 0
    kept = rs1_sum[pl.ds(pl.multiple_of(32 * core, 32), 32), :]
    swapped = rs2_swap[...]
    sides = (jnp.where(is_first, kept, swapped), jnp.where(is_first, swapped, kept))
    for step in range(CHIPS // 2):
        for part in range(4):
            piece_4 = sides[part // 2][4 * step : 4 * step + 4, 128 * (part % 2) : 128 * (part % 2) + 128]
            rs2_rows[16 * step + 4 * part : 16 * step + 4 * part + 4, :] = piece_4
    rs2_send[...] = rs2_rows[...].astype(BF16)

    summing = core == near

    @pl.when(summing)
    def _():
        pltpu.make_async_copy(part_16(rs2_send, eight), part_16(rs2_recv, chip), sems.at[23]).start()

    @pl.when(jnp.logical_not(summing))
    def _():
        pltpu.make_async_remote_copy(
            src_ref=part_16(rs2_send, eight), dst_ref=part_16(rs2_recv, chip),
            send_sem=sems.at[22], recv_sem=sems.at[23],
            device_id=(grp, (8 * core + eight) * 2 + core), device_id_type=MESH,
        ).start()

    @pl.loop(1, 8)
    def _(step):
        peer = lax.rem(eight + step, 8)
        pltpu.make_async_remote_copy(
            src_ref=part_16(rs2_send, peer), dst_ref=part_16(rs2_recv, chip),
            send_sem=sems.at[22], recv_sem=sems.at[23],
            device_id=(grp, (8 * core + peer) * 2 + core), device_id_type=MESH,
        ).start()

    exchange(7, 4, 4)

    mixed_o[...] = put_back(5).astype(BF16)
    gq_o[...] = (stop_q[...] + put_back(6)).astype(BF16)

    give = pltpu.make_async_remote_copy(
        src_ref=rs3_send, dst_ref=rs3_recv, send_sem=sems.at[2], recv_sem=sems.at[3],
        device_id=(grp, sibling), device_id_type=MESH,
    )

    @pl.when(summing)
    def _():
        wait_for(rs2_recv, 23)
        rows_16 = jnp.sum(rs2_recv[...].astype(F32).reshape(CHIPS, 16, 128), axis=0)
        rs3_rows[...] = rows_16 * ((R * MEMBERS * GROUPS) ** -0.5)
        four = [rs3_rows[4 * part : 4 * part + 4, :] for part in range(4)]
        rows_4 = jnp.concatenate(four, axis=1)
        rs3_send[...] = jnp.where(is_first, rows_4[2:4], rows_4[0:2])
        give.start()
        gw_o[...] = jnp.where(is_first, rows_4[0:2], rows_4[2:4])

    gk_o[...] = (stop_k[...] + put_back(7)).astype(BF16)

    @pl.when(summing)
    def _():
        give.wait_send()

    @pl.when(jnp.logical_not(summing))
    def _():
        give.wait_recv()
        gw_o[...] = rs3_recv[...]

    for number in range(8):
        sent(number)
    wait_for(send_m.at[pl.ds(0, MEMBERS - 1)], 4)
    wait_for(w_send, 8)

    @pl.when(core == 0)
    def _():
        wait_for(w_send, 8)

    wait_for(w_recv.at[:, pl.ds(0, 3)], 24)
    wait_for(rs1_send.at[pl.ds(0, GROUPS - 1)], 18)
    wait_for(rs2_send.at[pl.ds(0, 7 * 16)], 22)

    @pl.when(jnp.logical_not(summing))
    def _():
        wait_for(rs2_send.at[pl.ds(0, 16)], 22)


def write(*refs):
    *pairs, sems = refs
    copies = [
        pltpu.make_async_copy(source, target, sems.at[number])
        for number, (source, target) in enumerate(zip(pairs[:5], pairs[5:]))
    ]
    for copy in copies:
        copy.start()
    for copy in copies:
        copy.wait()


def shards(features, query_rows, key_rows, w_value, cotangent, station, bucket, slot_index):
    half = HD // 2
    vmem = pl.BlockSpec(memory_space=pltpu.VMEM)

    def buffer(shape, dtype):
        return pltpu.VMEM(shape, dtype)

    scratch = [
        buffer((R, D), BF16), buffer((R, HD), BF16), buffer((R, HD), BF16), buffer((2, HD), BF16), buffer((R, HD), BF16),
        buffer((1, R), I32), buffer((1, R), I32), buffer((1, R), I32),
        buffer((R, R), BF16), buffer((R, R), BF16), buffer((R, R), F32),
        buffer((HEADS, R, R), BF16), buffer((HEADS, R, R), BF16),
        buffer((8, 2 * R, half), BF16), buffer((8, 2 * R, half), BF16),
        buffer((MEMBERS, 1, 128), I32), buffer((MEMBERS, 1, 128), I32),
        buffer((2, 2, HD), F32), buffer((16, 128), F32), buffer((16, 128), BF16), buffer((2, 4, 16, 128), BF16),
        buffer((32, HD), F32), buffer((GROUPS, 2, 32, HD), BF16),
        buffer((R, HD), BF16), buffer((R, HD), BF16), buffer((R, HD), BF16), buffer((R, HD), BF16),
        buffer((R, HD), F32), buffer((R, HD), F32),
        buffer((R, HD), BF16), buffer((R, HD), BF16), buffer((R, HD), BF16), buffer((R, HD), BF16),
        buffer((R, HD), F32), buffer((R, HD), F32), buffer((R, HD), F32),
        buffer((D, half), F32), buffer((D, half), BF16), buffer((D, half), BF16),
        buffer((GROUPS, 64, half), BF16), buffer((GROUPS, 64, half), BF16),
        buffer((64, half), F32), buffer((32, half), F32), buffer((128, 128), F32), buffer((128, 128), BF16),
        buffer((R, 128), BF16), buffer((16, 128), F32), buffer((2, HD), F32), buffer((2, HD), F32),
        pltpu.SemaphoreType.DMA((26,)), pltpu.SemaphoreType.DMA((8,)),
        pltpu.SemaphoreType.DMA((8,)), pltpu.SemaphoreType.DMA((8,)), pltpu.SemaphoreType.REGULAR((2,)),
    ]
    kinds = (((R, HD), BF16), ((R, D), BF16), ((R, HD), BF16), ((R, HD), BF16), ((2, HD), F32))
    inputs = (
        features, query_rows, key_rows, w_value, cotangent,
        station.reshape(1, R), bucket.reshape(1, R), slot_index.reshape(1, R),
    )
    results = pl.pallas_call(
        kernel,
        out_shape=tuple(pltpu.VMEM(*kind) for kind in kinds),
        in_specs=[pl.BlockSpec(memory_space=pltpu.HBM)] * 8,
        out_specs=(vmem,) * 5,
        scratch_shapes=scratch,
        compiler_params=pltpu.CompilerParams(
            collective_id=0, has_side_effects=True, vmem_limit_bytes=48 * 1024 * 1024
        ),
        name="delay_attention",
    )(*(pltpu.with_memory_space_constraint(array, pltpu.HBM) for array in inputs))
    return pl.pallas_call(
        write,
        out_shape=tuple(jax.ShapeDtypeStruct(*kind) for kind in kinds),
        in_specs=[vmem] * 5,
        out_specs=(pl.BlockSpec(memory_space=pltpu.HBM),) * 5,
        scratch_shapes=[pltpu.SemaphoreType.DMA((5,))],
        name="write_results",
    )(*(pltpu.with_memory_space_constraint(array, pltpu.VMEM) for array in results))


def solution(mesh):
    rows = P(("grp", "trn"), None)
    ids = P(("grp", "trn"))
    return jax.shard_map(
        shards,
        mesh=mesh,
        in_specs=(rows,) * 5 + (ids,) * 3,
        out_specs=(rows,) * 5,
        check_vma=False,
    )
```
